512 devices in a mesh: ctx: 64 (over y, x, core), kvh: 8 (over z).
Axes of the slice: x: 4, y: 8, z: 8, core: 2. Of those that a mesh axis runs over, the one named last changes fastest.
Arguments:
- queries: bfloat16 [24576, 4096], P('ctx', 'kvh'), may hold values from -200 to 200
- key_head_rows: bfloat16 [24576, 1024], P('ctx', 'kvh'), may hold values from -6 to 6
- value_head_rows: bfloat16 [24576, 1024], P('ctx', 'kvh'), may hold values from -6 to 6
- output_cotangent: bfloat16 [24576, 4096], P('ctx', 'kvh'), may hold values from -6 to 6
- projection_input: bfloat16 [24576, 8192], P('ctx', 'kvh'), may hold values from -6 to 6
- adapter_hidden_state: bfloat16 [24576, 64], P('ctx'), may hold values from -6 to 6
- adapter_up_weight: bfloat16 [64, 4096], P(None, 'kvh'), may hold values from -0.09375 to 0.09375
- document_block_lengths: int32 [32], replicated, may hold values from 1 to 12, 192 in all
Outputs:
- query_gradient: bfloat16 [24576, 4096], P('ctx', 'kvh')
- key_gradient: bfloat16 [24576, 1024], P('ctx', 'kvh')
- value_gradient: bfloat16 [24576, 1024], P('ctx', 'kvh')
- down_adapter_gradient: float32 [8192, 64], P('kvh')
- up_adapter_gradient: float32 [64, 4096], P(None, 'kvh')
The draws below stay inside these ranges and needn't reach their ends.
Inputs may be any that keep to these rules, and one draw needn't show every extreme that they name: `document_block_lengths`: they sum to 192, and the longest document is exactly 12 blocks.
All inputs are finite; a program needn't handle non-finite values.
Results may differ from the reference program's by a relative error of at most 0.015.
Values may be sent and summed in bfloat16 or wider, within the bound.
A program may use at most 128 MiB of HBM per device.

```python
import math
import jax
import jax.numpy as jnp
import numpy as np
from jax import lax

HEAD_DIMENSION = 128
KEY_VALUE_HEADS = 8
DM = 8192
QUERY_PER_KEY = 4
ADAPTER_RANK = 64
REACH = 4
BLOCK = 128
TOK_DEV = 384
PACKED_TOKENS = 24576
DOCS = 32
N_CTX = 64


def shared_parts(key):
    base = jnp.clip(jax.random.normal(key, (PACKED_TOKENS, KEY_VALUE_HEADS, HEAD_DIMENSION), jnp.float32), -6.0, 6.0)
    return base


def draw_key_head_rows(key, part):
    base = shared_parts(key)
    return base.reshape(PACKED_TOKENS, KEY_VALUE_HEADS * HEAD_DIMENSION).astype(jnp.bfloat16)


def draw_queries(key, part):
    key = jax.random.fold_in(key, 9)
    drawn = jnp.clip(jax.random.normal(key, (PACKED_TOKENS, KEY_VALUE_HEADS, QUERY_PER_KEY, HEAD_DIMENSION), jnp.float32), -6.0, 6.0)
    return drawn.reshape(PACKED_TOKENS, KEY_VALUE_HEADS * QUERY_PER_KEY * HEAD_DIMENSION).astype(jnp.bfloat16)


def shard_levels(key, shape, cuts, low, largest):
    def one(axis_at, blocks):
        steps = jax.random.uniform(jax.random.fold_in(jax.random.fold_in(key, 6), axis_at), (blocks,), jnp.float32, low / len(cuts), largest / len(cuts))
        return jnp.repeat(jnp.exp(steps), shape[axis_at] // blocks).reshape((-1,) + (1,) * (len(shape) - axis_at - 1))

    level = one(*cuts[0])
    for cut in cuts[1:]:
        level = level * one(*cut)
    return level


def length_profile(number_of, total, limit, slope):
    loads = [(1 << 20) // math.isqrt(grade ** slope) + 1 for grade in range(2, number_of + 1)]
    spare, counts = total - limit - (number_of - 1), [1] * (number_of - 1)
    while spare > 0:
        movable = [i for i in range(number_of - 1) if counts[i] < limit]
        mass, remaining = sum([loads[i] for i in movable]), spare
        for i in movable:
            addition = min(limit - counts[i], max(1, remaining * loads[i] // mass), spare)
            counts[i] = counts[i] + addition
            spare = spare - addition
    return np.array([limit] + counts)


def ragged_sizes(own_key, amount, total, bound, skew):
    if amount == 2:
        one = jax.random.randint(own_key, (), max(1, total - bound), min(bound, total - 1) + 1)
        return jnp.stack([one, total - one])
    sizes = jnp.asarray(length_profile(amount, total, bound, skew), jnp.int32)
    twos = (amount - 1) // 2
    source_of, taker = sizes[1:1 + 2 * twos:2], sizes[2:2 + 2 * twos:2]
    slack = jnp.minimum(source_of - 1, bound - taker)
    moved = jax.random.randint(jax.random.fold_in(own_key, 1), (twos,), 0, 1 << 20) % (slack + 1)
    sizes = sizes.at[1:1 + 2 * twos:2].set(source_of - moved).at[2:2 + 2 * twos:2].set(taker + moved)
    return sizes[jax.random.permutation(jax.random.fold_in(own_key, 2), amount)]


def normal_values(rng, extent, deviation, reach, split=(), held_as=jnp.bfloat16):
    entries = deviation * jax.random.normal(rng, extent, jnp.float32)
    if split:
        entries = entries * shard_levels(rng, extent, split, -0.22, 0.18)
    return jnp.clip(entries, -reach, reach).astype(held_as)


def setup_inputs(seed: int = 0) -> dict:
    splits = jax.random.split(jax.random.key(seed), 9)
    queries = draw_queries(jax.random.fold_in(splits[8], 71), 0)
    key_head_rows = draw_key_head_rows(jax.random.fold_in(splits[8], 71), 0)
    value_head_rows = normal_values(splits[2], (PACKED_TOKENS, KEY_VALUE_HEADS * HEAD_DIMENSION), 1.0, 6.0, ((0, 64), (1, 8)))
    output_cotangent = normal_values(splits[3], (PACKED_TOKENS, KEY_VALUE_HEADS * QUERY_PER_KEY * HEAD_DIMENSION), 1.0, 6.0, ((0, 64), (1, 8)))
    projection_input = normal_values(splits[4], (PACKED_TOKENS, DM), 1.0, 6.0, ((0, 64), (1, 8)))
    adapter_hidden_state = normal_values(splits[5], (PACKED_TOKENS, ADAPTER_RANK), 1.0, 6.0, ((0, 64),))
    adapter_up_weight = normal_values(splits[6], (ADAPTER_RANK, KEY_VALUE_HEADS * QUERY_PER_KEY * HEAD_DIMENSION), (KEY_VALUE_HEADS * QUERY_PER_KEY * HEAD_DIMENSION) ** -0.5, 0.09375, ((1, 8),))
    document_block_lengths = ragged_sizes(splits[7], DOCS, PACKED_TOKENS // BLOCK, REACH * TOK_DEV // BLOCK, 2).astype(jnp.int32)
    return {"queries": queries, "key_head_rows": key_head_rows, "value_head_rows": value_head_rows, "output_cotangent": output_cotangent, "projection_input": projection_input, "adapter_hidden_state": adapter_hidden_state, "adapter_up_weight": adapter_up_weight, "document_block_lengths": document_block_lengths}


def doc_start(positions, document_block_lengths):
    offsets = (BLOCK * (jnp.cumsum(document_block_lengths) - document_block_lengths)).astype(jnp.int32)
    chosen = jnp.where(offsets[None, :] <= positions[:, None], offsets[None, :], jnp.zeros((), jnp.int32))
    return jnp.max(chosen, axis=1).astype(jnp.int32)


def reference(queries, key_head_rows, value_head_rows, output_cotangent, projection_input, adapter_hidden_state, adapter_up_weight, document_block_lengths):
    span_rows = (REACH + 1) * TOK_DEV
    factor = HEAD_DIMENSION ** -0.5
    query_h = queries.reshape(PACKED_TOKENS, KEY_VALUE_HEADS, QUERY_PER_KEY, HEAD_DIMENSION)
    grad_out = output_cotangent.reshape(PACKED_TOKENS, KEY_VALUE_HEADS, QUERY_PER_KEY, HEAD_DIMENSION)
    padding = jnp.zeros((REACH * TOK_DEV, KEY_VALUE_HEADS, HEAD_DIMENSION), jnp.bfloat16)
    key_pad = jnp.concatenate([padding, key_head_rows.reshape(PACKED_TOKENS, KEY_VALUE_HEADS, HEAD_DIMENSION)], axis=0)
    value_pad = jnp.concatenate([padding, value_head_rows.reshape(PACKED_TOKENS, KEY_VALUE_HEADS, HEAD_DIMENSION)], axis=0)
    first_all = doc_start(jnp.arange(PACKED_TOKENS, dtype=jnp.int32), document_block_lengths)
    zero_index = jnp.zeros((), jnp.int32)

    def one_block(grad_window, block_index):
        first_row = (block_index * TOK_DEV).astype(jnp.int32)
        query_tile = lax.dynamic_slice_in_dim(query_h, first_row, TOK_DEV, 0).astype(jnp.float32)
        out_tile = lax.dynamic_slice_in_dim(grad_out, first_row, TOK_DEV, 0).astype(jnp.float32)
        key_tile = lax.dynamic_slice_in_dim(key_pad, first_row, span_rows, 0).astype(jnp.float32)
        value_tile = lax.dynamic_slice_in_dim(value_pad, first_row, span_rows, 0).astype(jnp.float32)
        query_pos = first_row + jnp.arange(TOK_DEV, dtype=jnp.int32)
        key_pos = first_row - REACH * TOK_DEV + jnp.arange(span_rows, dtype=jnp.int32)
        first_pos = lax.dynamic_slice_in_dim(first_all, first_row, TOK_DEV, 0)
        allowed = (key_pos[None, :] <= query_pos[:, None]) & (key_pos[None, :] >= first_pos[:, None])
        allowed = allowed[:, None, None, :]
        scores = jnp.einsum("tghd,sgd->tghs", query_tile, key_tile) * factor
        masked = jnp.where(allowed, scores, -jnp.inf)
        row_max = jnp.max(masked, axis=3, keepdims=True)
        log_total = row_max + jnp.log(jnp.sum(jnp.exp(masked - row_max), axis=3, keepdims=True))
        prob_tile = jnp.where(allowed, jnp.exp(scores - log_total), 0.0)
        dprob_tile = jnp.einsum("tghd,sgd->tghs", out_tile, value_tile)
        row_delta = jnp.sum(prob_tile * dprob_tile, axis=3, keepdims=True)
        dscore = lax.optimization_barrier((prob_tile * (dprob_tile - row_delta)).astype(jnp.bfloat16)).astype(jnp.float32)
        prob_low = lax.optimization_barrier(prob_tile.astype(jnp.bfloat16)).astype(jnp.float32)
        grad_query = jnp.einsum("tghs,sgd->tghd", dscore, key_tile) * factor
        grad_key = jnp.einsum("tghs,tghd->sgd", dscore, query_tile) * factor
        grad_value = jnp.einsum("tghs,tghd->sgd", prob_low, out_tile)
        corner = (zero_index, first_row, zero_index, zero_index)
        current = lax.dynamic_slice(grad_window, corner, (2, span_rows, KEY_VALUE_HEADS, HEAD_DIMENSION))
        grad_window = lax.dynamic_update_slice(grad_window, current + jnp.stack([grad_key, grad_value]), corner)
        return grad_window, grad_query.astype(jnp.bfloat16)

    grad_window = jnp.zeros((2, PACKED_TOKENS + REACH * TOK_DEV, KEY_VALUE_HEADS, HEAD_DIMENSION), jnp.float32)
    grad_window, grad_tiles = lax.scan(one_block, grad_window, jnp.arange(N_CTX, dtype=jnp.int32))
    query_gradient = grad_tiles.reshape(PACKED_TOKENS, KEY_VALUE_HEADS * QUERY_PER_KEY * HEAD_DIMENSION)
    key_gradient = grad_window[0, REACH * TOK_DEV:].astype(jnp.bfloat16).reshape(PACKED_TOKENS, KEY_VALUE_HEADS * HEAD_DIMENSION)
    value_gradient = grad_window[1, REACH * TOK_DEV:].astype(jnp.bfloat16).reshape(PACKED_TOKENS, KEY_VALUE_HEADS * HEAD_DIMENSION)
    blended_output = jnp.dot(query_gradient, adapter_up_weight.T, preferred_element_type=jnp.float32)
    blended_output_lowp = blended_output.astype(jnp.bfloat16)
    scale_norm_divisor = PACKED_TOKENS ** -0.5
    down_adapter_gradient = jnp.dot(projection_input.T, blended_output_lowp, preferred_element_type=jnp.float32) * scale_norm_divisor
    up_adapter_gradient = jnp.dot(adapter_hidden_state.T, query_gradient, preferred_element_type=jnp.float32) * scale_norm_divisor
    return (query_gradient, key_gradient, value_gradient, down_adapter_gradient, up_adapter_gradient)
```

```python
import functools
import math

import jax
import jax.numpy as jnp
from jax import lax
from jax.experimental import pallas as pl
from jax.experimental.pallas import tpu as pltpu
from jax.sharding import PartitionSpec as P

MESH = pl.DeviceIdType.MESH
HEAD = 128
HEADS = 4
BLOCK = 128
REACH = 4
TOK = 384
PER = TOK // BLOCK
SPAN = 12
ROWS = HEADS * BLOCK
NX, NCORE = 4, 2
FAR = 1e30
BF = jnp.bfloat16
F32 = jnp.float32

NT = (((1,), (1,)), ((), ()))
NN = (((1,), (0,)), ((), ()))


def dot(a, b, dims=NN):
    return lax.dot_general(a, b, dims, preferred_element_type=F32)


def fold8(tile, op):
    parts = tile.reshape(tile.shape[0] // 8, 8, tile.shape[1])
    return op(parts, axis=0)


def kernel(
    n_ctx, n_kvh, q_hbm, k_hbm, v_hbm, g_hbm, x_hbm, a_hbm, w_hbm, len_hbm,
    qg_hbm, dk_hbm, dv_hbm, down_hbm, up_hbm,
    q_ref, g_ref, x_ref, a_ref, w_ref, len_ref, kwin, vwin, kwin_t, s_ref, dp_ref, p_ref, ds_ref,
    top_ref, qg_ref, back_k, back_v, got_k, got_v, dk_ref, dv_ref,
    mix_own, mix_send, mix_got,
    down_own, up_own, down_send, up_send, down_a, up_a, down_y, up_y, down_fin, up_fin, down_out, up_out,
    in_sem, out_sem, halo_s, halo_r, back_s, back_r, mix_s, mix_r, rs_s, rs_r, ys_s, ys_r, ag_s, ag_r,
):
    n_y = n_ctx // (NX * NCORE)
    c = lax.axis_index("ctx")
    z = lax.axis_index("kvh")
    core = lax.rem(c, NCORE)
    x = lax.rem(c // NCORE, NX)
    y = c // (NX * NCORE)

    def at(yy, xx, cc):
        return ((yy * NX + xx) * NCORE + cc, z)

    def along(d):
        return (lax.rem(c + d + n_ctx, n_ctx), z)

    z_peers = [(lax.rem(z + o, n_kvh)) for o in range(1, n_kvh)]
    y_peers = [lax.rem(y + o, n_y) for o in range(1, n_y)]
    a_peers = [
        (lax.rem(x + dx, NX), lax.rem(core + dc, NCORE))
        for dx in range(NX) for dc in range(NCORE) if (dx, dc) != (0, 0)
    ]

    own = pl.ds(REACH * TOK, TOK)
    local = [
        pltpu.make_async_copy(src, dst, in_sem.at[i])
        for i, (src, dst) in enumerate([
            (q_hbm, q_ref), (k_hbm, kwin.at[own]), (g_hbm, g_ref), (v_hbm, vwin.at[own]),
            (len_hbm, len_ref), (w_hbm, w_ref), (a_hbm, a_ref), (x_hbm, x_ref),
        ])
    ]
    for cp in local:
        cp.start()
    lq, lk, lg, lv, llen, lw, la, lx = local

    barrier = pltpu.get_barrier_semaphore()
    greet = [along(d) for d in range(1, REACH + 1)] + [along(-d) for d in range(1, REACH + 1)]
    greet += [(c, zz) for zz in z_peers]
    greet += [at(yy, x, core) for yy in y_peers]
    greet += [at(y, xx, cc) for xx, cc in a_peers]
    for who in greet:
        pl.semaphore_signal(barrier, inc=1, device_id=who, device_id_type=MESH)
    pl.semaphore_wait(barrier, len(greet))

    halo = {}
    for d in range(1, REACH + 1):
        first = BLOCK if d == REACH else 0
        for j, (src, win) in enumerate([(k_hbm, kwin), (v_hbm, vwin)]):
            cp = pltpu.make_async_remote_copy(
                src_ref=src.at[pl.ds(first, TOK - first)],
                dst_ref=win.at[pl.ds((REACH - d) * TOK + first, TOK - first)],
                send_sem=halo_s.at[d - 1, j], recv_sem=halo_r.at[d - 1, j],
                device_id=along(d), device_id_type=MESH,
            )
            cp.start()
            halo[d, j] = cp

    llen.wait()
    firsts = [jnp.int32(0)] * PER
    start = jnp.int32(0)
    for doc in range(len_hbm.shape[0]):
        for i in range(PER):
            firsts[i] = jnp.where(start <= c * PER + i, start, firsts[i])
        start = start + len_ref[doc]

    def away(i, slot):
        block = c * PER + i + slot - (SPAN - 1)
        return jnp.where(block >= firsts[i], 0.0, FAR).astype(F32)

    def rows_of(ref, i):
        return jnp.concatenate(
            [ref[i * BLOCK:(i + 1) * BLOCK, h * HEAD:(h + 1) * HEAD] for h in range(HEADS)], axis=0
        )

    for i in range(PER):
        top_ref[i] = jnp.full((8, ROWS), -2.0 * FAR, F32)

    causal = (
        lax.broadcasted_iota(jnp.int32, (BLOCK, ROWS), 0)
        <= lax.broadcasted_iota(jnp.int32, (BLOCK, ROWS), 1) % BLOCK
    )

    def window(d, i):
        low = (REACH - d) * PER
        return max(low, i + 1), min(low + PER, i + SPAN + 1)

    def scores(d):
        for i in range(PER):
            lo, hi = window(d, i)
            if lo >= hi:
                continue
            s = dot(kwin[lo * BLOCK:hi * BLOCK], rows_of(q_ref, i), NT)
            top = top_ref[i]
            for w in range(lo, hi):
                slot = w - i - 1
                tile = s[(w - lo) * BLOCK:(w - lo + 1) * BLOCK]
                if slot == SPAN - 1:
                    tile = jnp.where(causal, tile, -FAR)
                s_ref[i, slot * BLOCK:(slot + 1) * BLOCK] = tile
                top = jnp.maximum(top, fold8(tile, jnp.max) - away(i, slot))
            top_ref[i] = top
        low = (REACH - d) * TOK + (BLOCK if d == REACH else 0)
        high = (REACH - d + 1) * TOK
        kwin_t[:, low:high] = kwin[low:high].T

    def dprobs(d):
        for i in range(PER):
            lo, hi = window(d, i)
            if lo >= hi:
                continue
            dp_ref[i, (lo - i - 1) * BLOCK:(hi - i - 1) * BLOCK] = dot(
                vwin[lo * BLOCK:hi * BLOCK], rows_of(g_ref, i), NT
            )

    lq.wait()
    lk.wait()
    scores(0)
    lg.wait()
    lv.wait()
    dprobs(0)
    for d in range(1, REACH + 1):
        halo[d, 0].wait_recv()
        scores(d)
        halo[d, 1].wait_recv()
        dprobs(d)

    factor = HEAD ** -0.5
    rate = factor * math.log2(math.e)
    STEP = 64
    lw.wait()
    mix_copies = []
    for i in range(PER):
        top = jnp.max(top_ref[i], axis=0, keepdims=True)

        def weigh(t, carry, i=i, top=top):
            total, delta = carry
            span = pl.ds(pl.multiple_of(t * STEP, STEP), STEP)
            level = top + away(i, t * STEP // BLOCK)
            p = jnp.exp2((s_ref[i, span] - level) * rate)
            s_ref[i, span] = p
            return total + fold8(p, jnp.sum), delta + fold8(p * dp_ref[i, span], jnp.sum)

        zero = jnp.zeros((8, ROWS), F32)
        total, delta = lax.fori_loop(0, SPAN * BLOCK // STEP, weigh, (zero, zero))
        share = 1.0 / jnp.sum(total, axis=0, keepdims=True)
        delta = jnp.sum(delta, axis=0, keepdims=True) * share

        def settle(t, carry, i=i, share=share, delta=delta):
            span = pl.ds(pl.multiple_of(t * STEP, STEP), STEP)
            p = s_ref[i, span] * share
            p_ref[i, span] = p.astype(BF)
            ds_ref[i, span] = (p * (dp_ref[i, span] - delta)).astype(BF)
            return carry

        lax.fori_loop(0, SPAN * BLOCK // STEP, settle, 0)
        dq = dot(kwin_t[:, (i + 1) * BLOCK:(i + 1 + SPAN) * BLOCK], ds_ref[i]) * factor
        for h in range(HEADS):
            qg_ref[i * BLOCK:(i + 1) * BLOCK, h * HEAD:(h + 1) * HEAD] = (
                dq[:, h * HEAD:(h + 1) * HEAD].T.astype(BF)
            )
        mixed = dot(w_ref[...], qg_ref[i * BLOCK:(i + 1) * BLOCK], NT)
        mix_own[:, i * BLOCK:(i + 1) * BLOCK] = mixed
        mix_send[i] = mixed.astype(BF)
        for o, zz in enumerate(z_peers):
            cp = pltpu.make_async_remote_copy(
                src_ref=mix_send.at[i], dst_ref=mix_got.at[i, o],
                send_sem=mix_s.at[i, o], recv_sem=mix_r.at[i, o],
                device_id=(c, zz), device_id_type=MESH,
            )
            cp.start()
            mix_copies.append(cp)

    out_qg = pltpu.make_async_copy(qg_ref, qg_hbm, out_sem.at[0])
    out_qg.start()

    def chunk(ref, xx, cc):
        width = ref.shape[1] // NCORE
        return ref.at[pl.ds(pl.multiple_of(xx * 16, 16), 16), pl.ds(pl.multiple_of(cc * width, 128), width)]

    def scatter(which, send, got):
        copies = []
        for o, (xx, cc) in enumerate(a_peers):
            cp = pltpu.make_async_remote_copy(
                src_ref=chunk(send, xx, cc), dst_ref=got.at[o],
                send_sem=rs_s.at[which, o], recv_sem=rs_r.at[which, o],
                device_id=at(y, xx, cc), device_id_type=MESH,
            )
            cp.start()
            copies.append(cp)
        return copies

    def exchange(which, copies, own_part, got, slots):
        for cp in copies:
            cp.wait_recv()
        part = chunk(own_part, x, core)[...]
        for o in range(len(a_peers)):
            part = part + got[o].astype(F32)
        slots[y] = part.astype(BF)
        out = []
        for o, yy in enumerate(y_peers):
            cp = pltpu.make_async_remote_copy(
                src_ref=slots.at[y], dst_ref=slots.at[y],
                send_sem=ys_s.at[which, o], recv_sem=ys_r.at[which, o],
                device_id=at(yy, x, core), device_id_type=MESH,
            )
            cp.start()
            out.append(cp)
        return out

    def gather(which, copies, slots, fin):
        for cp in copies:
            cp.wait_recv()
        part = slots[0].astype(F32)
        for yy in range(1, n_y):
            part = part + slots[yy].astype(F32)
        mine = chunk(fin, x, core)
        mine[...] = part.astype(BF)
        out = []
        for o, (xx, cc) in enumerate(a_peers):
            cp = pltpu.make_async_remote_copy(
                src_ref=mine, dst_ref=mine,
                send_sem=ag_s.at[which, o], recv_sem=ag_r.at[which, o],
                device_id=at(y, xx, cc), device_id_type=MESH,
            )
            cp.start()
            out.append(cp)
        return out

    la.wait()
    up = dot(a_ref[...], qg_ref[...])
    up_own[...] = up
    up_send[...] = up.astype(BF)
    up_rs = scatter(0, up_send, up_a)

    def ranges(d):
        low = (REACH - d) * PER
        dk = jnp.zeros((TOK, HEAD), F32)
        dv = jnp.zeros((TOK, HEAD), F32)
        parts_k, parts_v = [None] * PER, [None] * PER
        for i in range(PER):
            lo, hi = window(d, i)
            if lo >= hi:
                continue
            span = slice((lo - i - 1) * BLOCK, (hi - i - 1) * BLOCK)
            k_part = dot(ds_ref[i, span], rows_of(q_ref, i))
            v_part = dot(p_ref[i, span], rows_of(g_ref, i))
            for w in range(lo, hi):
                at_w = slice((w - lo) * BLOCK, (w - lo + 1) * BLOCK)
                b = w - low
                parts_k[b] = k_part[at_w] if parts_k[b] is None else parts_k[b] + k_part[at_w]
                parts_v[b] = v_part[at_w] if parts_v[b] is None else parts_v[b] + v_part[at_w]
        return parts_k, parts_v

    back = []
    for d in range(REACH, 0, -1):
        parts = ranges(d)
        first = BLOCK if d == REACH else 0
        for j, (buf, got) in enumerate([(back_k, got_k), (back_v, got_v)]):
            for b in range(first // BLOCK, PER):
                value = parts[j][b] * factor if j == 0 else parts[j][b]
                buf[d - 1, b * BLOCK:(b + 1) * BLOCK] = value.astype(BF)
            cp = pltpu.make_async_remote_copy(
                src_ref=buf.at[d - 1, pl.ds(first, TOK - first)],
                dst_ref=got.at[d - 1, pl.ds(first, TOK - first)],
                send_sem=back_s.at[d - 1, j], recv_sem=back_r.at[d - 1, j],
                device_id=along(-d), device_id_type=MESH,
            )
            cp.start()
            back.append(cp)

    up_ys = exchange(0, up_rs, up_own, up_a, up_y)

    parts_k, parts_v = ranges(0)

    for cp in mix_copies:
        cp.wait_recv()
    lx.wait()
    mixed = mix_own[...]
    for o in range(n_kvh - 1):
        mixed = mixed + jnp.concatenate([mix_got[i, o].astype(F32) for i in range(PER)], axis=1)
    down = dot(mixed.astype(BF), x_ref[...])
    down_own[...] = down
    down_send[...] = down.astype(BF)
    down_rs = scatter(1, down_send, down_a)

    up_ag = gather(0, up_ys, up_y, up_fin)
    down_ys = exchange(1, down_rs, down_own, down_a, down_y)

    for cp in back:
        cp.wait_recv()
    for b in range(PER):
        rows = slice(b * BLOCK, (b + 1) * BLOCK)
        sum_k, sum_v = parts_k[b] * factor, parts_v[b]
        for d in range(1, REACH + 1):
            if d == REACH and b == 0:
                continue
            sum_k = sum_k + got_k[d - 1, rows].astype(F32)
            sum_v = sum_v + got_v[d - 1, rows].astype(F32)
        dk_ref[rows] = sum_k.astype(BF)
        dv_ref[rows] = sum_v.astype(BF)
    out_dk = pltpu.make_async_copy(dk_ref, dk_hbm, out_sem.at[1])
    out_dv = pltpu.make_async_copy(dv_ref, dv_hbm, out_sem.at[2])
    out_dk.start()
    out_dv.start()

    down_ag = gather(1, down_ys, down_y, down_fin)
    scale = (TOK * n_ctx) ** -0.5
    for cp in up_ag:
        cp.wait_recv()
    up_out[...] = up_fin[...].astype(F32) * scale
    out_up = pltpu.make_async_copy(up_out, up_hbm, out_sem.at[3])
    out_up.start()
    for cp in down_ag:
        cp.wait_recv()
    down_out[...] = down_fin[...].astype(F32) * scale
    out_down = pltpu.make_async_copy(down_out, down_hbm, out_sem.at[4])
    out_down.start()

    for group in (list(halo.values()), back, mix_copies, up_rs, down_rs, up_ys, down_ys, up_ag, down_ag):
        for cp in group:
            cp.wait_send()
    for cp in (out_qg, out_dk, out_dv, out_up, out_down):
        cp.wait()


def shards(n_ctx, n_kvh, q, k, v, g, proj, hidden, weight, lengths):
    n_y = n_ctx // (NX * NCORE)
    n_a = NX * NCORE - 1
    feats, rank = proj.shape[1], hidden.shape[1]
    wide = q.shape[1]
    vm = pltpu.VMEM
    dma = pltpu.SemaphoreType.DMA
    win = (REACH + 1) * TOK
    anywhere = pl.BlockSpec(memory_space=pl.ANY)
    zs, ys = max(n_kvh - 1, 1), max(n_y - 1, 1)
    outs = pl.pallas_call(
        functools.partial(kernel, n_ctx, n_kvh),
        out_shape=(
            jax.ShapeDtypeStruct(q.shape, BF),
            jax.ShapeDtypeStruct(k.shape, BF),
            jax.ShapeDtypeStruct(v.shape, BF),
            jax.ShapeDtypeStruct((rank, feats), F32),
            jax.ShapeDtypeStruct((rank, wide), F32),
        ),
        in_specs=[anywhere] * 8,
        out_specs=(anywhere,) * 5,
        scratch_shapes=[
            vm(q.shape, BF), vm(g.shape, BF), vm(proj.shape, BF), vm((rank, TOK), BF), vm(weight.shape, BF),
            pltpu.SMEM(lengths.shape, jnp.int32),
            vm((win, HEAD), BF), vm((win, HEAD), BF), vm((HEAD, win), BF),
            vm((PER, SPAN * BLOCK, ROWS), F32), vm((PER, SPAN * BLOCK, ROWS), F32),
            vm((PER, SPAN * BLOCK, ROWS), BF), vm((PER, SPAN * BLOCK, ROWS), BF),
            vm((PER, 8, ROWS), F32), vm(q.shape, BF),
            vm((REACH, TOK, HEAD), BF), vm((REACH, TOK, HEAD), BF),
            vm((REACH, TOK, HEAD), BF), vm((REACH, TOK, HEAD), BF),
            vm(k.shape, BF), vm(v.shape, BF),
            vm((rank, TOK), F32), vm((PER, rank, BLOCK), BF), vm((PER, zs, rank, BLOCK), BF),
            vm((rank, feats), F32), vm((rank, wide), F32), vm((rank, feats), BF), vm((rank, wide), BF),
            vm((n_a, 16, feats // NCORE), BF), vm((n_a, 16, wide // NCORE), BF),
            vm((n_y, 16, feats // NCORE), BF), vm((n_y, 16, wide // NCORE), BF),
            vm((rank, feats), BF), vm((rank, wide), BF),
            vm((rank, feats), F32), vm((rank, wide), F32),
            dma((8,)), dma((5,)), dma((REACH, 2)), dma((REACH, 2)), dma((REACH, 2)), dma((REACH, 2)),
            dma((PER, zs)), dma((PER, zs)), dma((2, n_a)), dma((2, n_a)), dma((2, ys)), dma((2, ys)),
            dma((2, n_a)), dma((2, n_a)),
        ],
        compiler_params=pltpu.CompilerParams(
            collective_id=0, has_side_effects=True, vmem_limit_bytes=56 * 2**20
        ),
        cost_estimate=pl.CostEstimate(flops=3_200_000_000, bytes_accessed=4_000_000, transcendentals=2_400_000),
        name="attention_backward",
    )(q, k, v, g, proj, hidden.T, weight, lengths)
    qg, dk, dv, down, up = outs
    return qg, dk, dv, down.T, up


def solution(mesh):
    n_ctx, n_kvh = mesh.shape["ctx"], mesh.shape["kvh"]
    both = P("ctx", "kvh")
    return jax.shard_map(
        functools.partial(shards, n_ctx, n_kvh),
        mesh=mesh,
        in_specs=(both, both, both, both, both, P("ctx", None), P(None, "kvh"), P()),
        out_specs=(both, both, both, P("kvh", None), P(None, "kvh")),
        check_vma=False,
    )
```

```python
import functools
import math

import jax
import jax.numpy as jnp
from jax import lax
from jax.experimental import pallas as pl
from jax.experimental.pallas import tpu as pltpu
from jax.sharding import PartitionSpec as P

MESH = pl.DeviceIdType.MESH
HEAD = 128
HEADS = 4
BLOCK = 128
REACH = 4
TOK = 384
PER = TOK // BLOCK
SPAN = 12
ROWS = HEADS * BLOCK
NX, NCORE = 4, 2
FAR = 1e30
BF = jnp.bfloat16
F32 = jnp.float32

NT = (((1,), (1,)), ((), ()))
NN = (((1,), (0,)), ((), ()))


def dot(a, b, dims=NN):
    return lax.dot_general(a, b, dims, preferred_element_type=F32)


def fold8(tile, op):
    parts = tile.reshape(tile.shape[0] // 8, 8, tile.shape[1])
    return op(parts, axis=0)


def kernel(
    n_ctx, n_kvh, q_hbm, k_hbm, v_hbm, g_hbm, x_hbm, a_hbm, w_hbm, len_hbm,
    qg_ref, dk_ref, dv_ref, down_out, up_out,
    q_ref, g_ref, x_ref, a_ref, w_ref, len_ref, kwin, vwin, kwin_t, s_ref, dp_ref, p_ref, ds_ref,
    top_ref, near, back, got,
    mix_own, mix_send, mix_got,
    down_own, up_own, down_send, up_send, down_a, up_a, down_y, up_y, down_fin, up_fin,
    in_sem, halo_s, halo_r, back_s, back_r, mix_s, mix_r, rs_s, rs_r, ys_s, ys_r, ag_s, ag_r,
):
    n_y = n_ctx // (NX * NCORE)
    c = lax.axis_index("ctx")
    z = lax.axis_index("kvh")
    core = lax.rem(c, NCORE)
    x = lax.rem(c // NCORE, NX)
    y = c // (NX * NCORE)

    def at(yy, xx, cc):
        return ((yy * NX + xx) * NCORE + cc, z)

    def along(d):
        return (lax.rem(c + d + n_ctx, n_ctx), z)

    z_peers = [(lax.rem(z + o, n_kvh)) for o in range(1, n_kvh)]
    y_peers = [lax.rem(y + o, n_y) for o in range(1, n_y)]
    a_peers = [
        (lax.rem(x + dx, NX), lax.rem(core + dc, NCORE))
        for dx in range(NX) for dc in range(NCORE) if (dx, dc) != (0, 0)
    ]

    own = pl.ds(REACH * TOK, TOK)
    local = [
        pltpu.make_async_copy(src, dst, in_sem.at[i])
        for i, (src, dst) in enumerate([
            (q_hbm, q_ref), (k_hbm, kwin.at[own]), (g_hbm, g_ref), (v_hbm, vwin.at[own]),
            (len_hbm, len_ref), (w_hbm, w_ref), (a_hbm, a_ref), (x_hbm, x_ref),
        ])
    ]
    for cp in local:
        cp.start()
    lq, lk, lg, lv, llen, lw, la, lx = local

    barrier = pltpu.get_barrier_semaphore()
    greet = [along(d) for d in (1, 2, 3, -1, -2, -3)]
    greet += [(c, zz) for zz in z_peers]
    greet += [at(yy, x, core) for yy in y_peers]
    greet += [at(y, xx, cc) for xx, cc in a_peers]
    for who in greet:
        pl.semaphore_signal(barrier, inc=1, device_id=who, device_id_type=MESH)
    pl.semaphore_wait(barrier, len(greet))

    mate = along(1 - 2 * core)
    first_core, second_core = core == 0, core == 1

    def slot_rows(d, first=0):
        return pl.ds((REACH - d) * TOK + first, TOK - first)

    def forward(n, j, src, d, to, first=0):
        return pltpu.make_async_remote_copy(
            src_ref=src, dst_ref=(kwin, vwin)[j].at[slot_rows(d, first)],
            send_sem=halo_s.at[n, j], recv_sem=halo_r.at[d - 1, j], device_id=to, device_id_type=MESH,
        )

    def held(j, d, first=0):
        return (kwin, vwin)[j].at[slot_rows(d, first)]

    def own_next(j):
        return forward(0, j, (k_hbm, v_hbm)[j], 1, along(1))

    def own_far(j):
        return forward(1, j, (k_hbm, v_hbm)[j], 3, along(3))

    def pass_mate(j, d):
        return forward(2, j, held(j, d), 2, mate)

    def pass_chip(j):
        return forward(3, j, held(j, 1), 3, along(2))

    def pass_last(j):
        return forward(4, j, held(j, 3, BLOCK), REACH, along(1), BLOCK)

    def arrived(j, d):
        first = BLOCK if d == REACH else 0
        forward(0, j, held(j, d, first), d, along(1), first).wait_recv()

    for j in range(2):
        own_next(j).start()

        @pl.when(first_core)
        def _(j=j):
            own_far(j).start()

    llen.wait()
    firsts = [jnp.int32(0)] * PER
    start = jnp.int32(0)
    for doc in range(len_hbm.shape[0]):
        for i in range(PER):
            firsts[i] = jnp.where(start <= c * PER + i, start, firsts[i])
        start = start + len_ref[doc]

    def away(i, slot):
        block = c * PER + i + slot - (SPAN - 1)
        return jnp.where(block >= firsts[i], 0.0, FAR).astype(F32)

    def rows_of(ref, i):
        return jnp.concatenate(
            [ref[i * BLOCK:(i + 1) * BLOCK, h * HEAD:(h + 1) * HEAD] for h in range(HEADS)], axis=0
        )

    for i in range(PER):
        top_ref[i] = jnp.full((8, ROWS), -2.0 * FAR, F32)

    causal = (
        lax.broadcasted_iota(jnp.int32, (BLOCK, ROWS), 0)
        <= lax.broadcasted_iota(jnp.int32, (BLOCK, ROWS), 1) % BLOCK
    )

    def window(d, i):
        low = (REACH - d) * PER
        return max(low, i + 1), min(low + PER, i + SPAN + 1)

    def scores(d):
        for i in range(PER):
            lo, hi = window(d, i)
            if lo >= hi:
                continue
            s = dot(kwin[lo * BLOCK:hi * BLOCK], rows_of(q_ref, i), NT)
            top = top_ref[i]
            for w in range(lo, hi):
                slot = w - i - 1
                tile = s[(w - lo) * BLOCK:(w - lo + 1) * BLOCK]
                if slot == SPAN - 1:
                    tile = jnp.where(causal, tile, -FAR)
                s_ref[i, slot * BLOCK:(slot + 1) * BLOCK] = tile
                top = jnp.maximum(top, fold8(tile, jnp.max) - away(i, slot))
            top_ref[i] = top
        low = (REACH - d) * TOK + (BLOCK if d == REACH else 0)
        high = (REACH - d + 1) * TOK
        kwin_t[:, low:high] = kwin[low:high].T

    def dprobs(d):
        for i in range(PER):
            lo, hi = window(d, i)
            if lo >= hi:
                continue
            dp_ref[i, (lo - i - 1) * BLOCK:(hi - i - 1) * BLOCK] = dot(
                vwin[lo * BLOCK:hi * BLOCK], rows_of(g_ref, i), NT
            )

    lq.wait()
    lk.wait()
    scores(0)
    lg.wait()
    lv.wait()
    dprobs(0)

    @pl.when(second_core)
    def _():
        for j in range(2):
            arrived(j, 1)
        scores(1)
        dprobs(1)
        for j in range(2):
            arrived(j, 3)
            pass_last(j).start()
            pass_mate(j, 3).start()
        scores(3)
        dprobs(3)

    @pl.when(first_core)
    def _():
        for j in range(2):
            arrived(j, 1)
            pass_chip(j).start()
            pass_mate(j, 1).start()
        scores(1)
        dprobs(1)

    for j in range(2):
        arrived(j, 2)
    scores(2)
    dprobs(2)

    @pl.when(first_core)
    def _():
        for j in range(2):
            arrived(j, 3)
            pass_last(j).start()
        scores(3)
        dprobs(3)

    arrived(0, REACH)
    scores(REACH)
    arrived(1, REACH)
    dprobs(REACH)

    factor = HEAD ** -0.5
    rate = factor * math.log2(math.e)
    STEP = 64
    lw.wait()
    mix_copies = []
    for i in range(PER):
        top = jnp.max(top_ref[i], axis=0, keepdims=True)

        def weigh(t, carry, i=i, top=top):
            total, delta = carry
            span = pl.ds(pl.multiple_of(t * STEP, STEP), STEP)
            level = top + away(i, t * STEP // BLOCK)
            p = jnp.exp2((s_ref[i, span] - level) * rate)
            s_ref[i, span] = p
            return total + fold8(p, jnp.sum), delta + fold8(p * dp_ref[i, span], jnp.sum)

        zero = jnp.zeros((8, ROWS), F32)
        total, delta = lax.fori_loop(0, SPAN * BLOCK // STEP, weigh, (zero, zero))
        share = 1.0 / jnp.sum(total, axis=0, keepdims=True)
        delta = jnp.sum(delta, axis=0, keepdims=True) * share

        def settle(t, carry, i=i, share=share, delta=delta):
            span = pl.ds(pl.multiple_of(t * STEP, STEP), STEP)
            p = s_ref[i, span] * share
            p_ref[i, span] = p.astype(BF)
            ds_ref[i, span] = (p * (dp_ref[i, span] - delta)).astype(BF)
            return carry

        lax.fori_loop(0, SPAN * BLOCK // STEP, settle, 0)
        dq = dot(kwin_t[:, (i + 1) * BLOCK:(i + 1 + SPAN) * BLOCK], ds_ref[i]) * factor
        for h in range(HEADS):
            qg_ref[i * BLOCK:(i + 1) * BLOCK, h * HEAD:(h + 1) * HEAD] = (
                dq[:, h * HEAD:(h + 1) * HEAD].T.astype(BF)
            )
        mixed = dot(w_ref[...], qg_ref[i * BLOCK:(i + 1) * BLOCK], NT)
        mix_own[:, i * BLOCK:(i + 1) * BLOCK] = mixed
        mix_send[i] = mixed.astype(BF)
        for o, zz in enumerate(z_peers):
            cp = pltpu.make_async_remote_copy(
                src_ref=mix_send.at[i], dst_ref=mix_got.at[i, o],
                send_sem=mix_s.at[i, o], recv_sem=mix_r.at[i, o],
                device_id=(c, zz), device_id_type=MESH,
            )
            cp.start()
            mix_copies.append(cp)

    def chunk(ref, xx, cc):
        width = ref.shape[1] // NCORE
        return ref.at[pl.ds(pl.multiple_of(xx * 16, 16), 16), pl.ds(pl.multiple_of(cc * width, 128), width)]

    def scatter(which, send, got):
        copies = []
        for o, (xx, cc) in enumerate(a_peers):
            cp = pltpu.make_async_remote_copy(
                src_ref=chunk(send, xx, cc), dst_ref=got.at[o],
                send_sem=rs_s.at[which, o], recv_sem=rs_r.at[which, o],
                device_id=at(y, xx, cc), device_id_type=MESH,
            )
            cp.start()
            copies.append(cp)
        return copies

    def exchange(which, copies, own_part, got, slots):
        for cp in copies:
            cp.wait_recv()
        part = chunk(own_part, x, core)[...]
        for o in range(len(a_peers)):
            part = part + got[o].astype(F32)
        slots[y] = part.astype(BF)
        out = []
        for o, yy in enumerate(y_peers):
            cp = pltpu.make_async_remote_copy(
                src_ref=slots.at[y], dst_ref=slots.at[y],
                send_sem=ys_s.at[which, o], recv_sem=ys_r.at[which, o],
                device_id=at(yy, x, core), device_id_type=MESH,
            )
            cp.start()
            out.append(cp)
        return out

    def gather(which, copies, slots, fin):
        for cp in copies:
            cp.wait_recv()
        part = slots[0].astype(F32)
        for yy in range(1, n_y):
            part = part + slots[yy].astype(F32)
        mine = chunk(fin, x, core)
        mine[...] = part.astype(BF)
        out = []
        for o, (xx, cc) in enumerate(a_peers):
            cp = pltpu.make_async_remote_copy(
                src_ref=mine, dst_ref=mine,
                send_sem=ag_s.at[which, o], recv_sem=ag_r.at[which, o],
                device_id=at(y, xx, cc), device_id_type=MESH,
            )
            cp.start()
            out.append(cp)
        return out

    la.wait()
    up = dot(a_ref[...], qg_ref[...])
    up_own[...] = up
    up_send[...] = up.astype(BF)
    up_rs = scatter(0, up_send, up_a)

    def ranges(d):
        low = (REACH - d) * PER
        dk = jnp.zeros((TOK, HEAD), F32)
        dv = jnp.zeros((TOK, HEAD), F32)
        parts_k, parts_v = [None] * PER, [None] * PER
        for i in range(PER):
            lo, hi = window(d, i)
            if lo >= hi:
                continue
            span = slice((lo - i - 1) * BLOCK, (hi - i - 1) * BLOCK)
            k_part = dot(ds_ref[i, span], rows_of(q_ref, i))
            v_part = dot(p_ref[i, span], rows_of(g_ref, i))
            for w in range(lo, hi):
                at_w = slice((w - lo) * BLOCK, (w - lo + 1) * BLOCK)
                b = w - low
                parts_k[b] = k_part[at_w] if parts_k[b] is None else parts_k[b] + k_part[at_w]
                parts_v[b] = v_part[at_w] if parts_v[b] is None else parts_v[b] + v_part[at_w]
        return parts_k, parts_v

    def store(d):
        parts = ranges(d)
        first = BLOCK if d == REACH else 0
        for j in range(2):
            for b in range(first // BLOCK, PER):
                value = parts[j][b] * factor if j == 0 else parts[j][b]
                near[d, j, b * BLOCK:(b + 1) * BLOCK] = value.astype(near.dtype)

    def send_back(n, src, slot, to, first=0):
        rows = pl.ds(first, TOK - first)
        return pltpu.make_async_remote_copy(
            src_ref=src.at[:, rows], dst_ref=got.at[slot, :, rows],
            send_sem=back_s.at[n], recv_sem=back_r.at[slot], device_id=to, device_id_type=MESH,
        )

    def came_back(slot, first=0):
        send_back(0, got.at[slot], slot, along(-1), first).wait_recv()

    back_4 = send_back(0, back.at[0], 0, along(-1), BLOCK)
    back_2 = send_back(1, back.at[1], 1, mate)
    back_1 = send_back(2, back.at[2], 2, along(-1))
    back_3 = send_back(2, back.at[2], 3, along(-2))
    last_0 = send_back(3, back.at[3], 4, along(-1))
    last_1 = send_back(3, back.at[3], 4, along(-3))

    store(REACH)
    back[0, :, BLOCK:] = near[REACH, :, BLOCK:].astype(BF)
    back_4.start()
    store(2)
    back[1] = near[2].astype(BF)
    back_2.start()
    store(1)
    store(3)

    @pl.when(second_core)
    def _():
        back[2] = near[1].astype(BF)
        back_1.start()

    @pl.when(first_core)
    def _():
        came_back(0, BLOCK)
        back[2, :, :BLOCK] = near[3, :, :BLOCK].astype(BF)
        back[2, :, BLOCK:] = (near[3, :, BLOCK:] + got[0, :, BLOCK:].astype(F32)).astype(BF)
        back_3.start()

    up_ys = exchange(0, up_rs, up_own, up_a, up_y)

    store(0)

    for cp in mix_copies:
        cp.wait_recv()
    lx.wait()
    mixed = mix_own[...]
    for o in range(n_kvh - 1):
        mixed = mixed + jnp.concatenate([mix_got[i, o].astype(F32) for i in range(PER)], axis=1)
    down = dot(mixed.astype(BF), x_ref[...])
    down_own[...] = down
    down_send[...] = down.astype(BF)
    down_rs = scatter(1, down_send, down_a)

    up_ag = gather(0, up_ys, up_y, up_fin)
    down_ys = exchange(1, down_rs, down_own, down_a, down_y)

    came_back(1)

    @pl.when(first_core)
    def _():
        came_back(3)
        back[3] = (near[1] + got[1].astype(F32) + got[3].astype(F32)).astype(BF)
        last_0.start()

    @pl.when(second_core)
    def _():
        came_back(0, BLOCK)
        back[3, :, :BLOCK] = (near[3, :, :BLOCK] + got[1, :, :BLOCK].astype(F32)).astype(BF)
        back[3, :, BLOCK:] = (
            near[3, :, BLOCK:] + got[1, :, BLOCK:].astype(F32) + got[0, :, BLOCK:].astype(F32)
        ).astype(BF)
        last_1.start()

    down_ag = gather(1, down_ys, down_y, down_fin)

    @pl.when(first_core)
    def _():
        came_back(2)
        near[0] = near[0] + got[2].astype(F32)

    came_back(4)
    dk_ref[...] = (near[0, 0] + got[4, 0].astype(F32)).astype(BF)
    dv_ref[...] = (near[0, 1] + got[4, 1].astype(F32)).astype(BF)

    scale = (TOK * n_ctx) ** -0.5
    for cp in up_ag:
        cp.wait_recv()
    up_out[...] = up_fin[...].astype(F32) * scale
    for cp in down_ag:
        cp.wait_recv()
    down_out[...] = down_fin[...].astype(F32) * scale

    @pl.when(first_core)
    def _():
        for j in range(2):
            own_far(j).wait_send()
            pass_chip(j).wait_send()
            pass_mate(j, 1).wait_send()
        back_3.wait_send()
        last_0.wait_send()

    @pl.when(second_core)
    def _():
        for j in range(2):
            pass_mate(j, 3).wait_send()
        back_1.wait_send()
        last_1.wait_send()

    for j in range(2):
        own_next(j).wait_send()
        pass_last(j).wait_send()
    back_4.wait_send()
    back_2.wait_send()
    for group in (mix_copies, up_rs, down_rs, up_ys, down_ys, up_ag, down_ag):
        for cp in group:
            cp.wait_send()


def hand_over(*refs):
    arrays, results, sem = refs[:5], refs[5:10], refs[10]
    out = [pltpu.make_async_copy(arrays[i], results[i], sem.at[i]) for i in range(5)]
    for cp in out:
        cp.start()
    for cp in out:
        cp.wait()


def shards(n_ctx, n_kvh, q, k, v, g, proj, hidden, weight, lengths):
    n_y = n_ctx // (NX * NCORE)
    n_a = NX * NCORE - 1
    feats, rank = proj.shape[1], hidden.shape[1]
    wide = q.shape[1]
    vm = pltpu.VMEM
    dma = pltpu.SemaphoreType.DMA
    win = (REACH + 1) * TOK
    anywhere = pl.BlockSpec(memory_space=pl.ANY)
    zs, ys = max(n_kvh - 1, 1), max(n_y - 1, 1)
    outs = pl.pallas_call(
        functools.partial(kernel, n_ctx, n_kvh),
        out_shape=(
            pltpu.VMEM(q.shape, BF),
            pltpu.VMEM(k.shape, BF),
            pltpu.VMEM(v.shape, BF),
            pltpu.VMEM((rank, feats), F32),
            pltpu.VMEM((rank, wide), F32),
        ),
        in_specs=[anywhere] * 8,
        out_specs=(pl.BlockSpec(memory_space=pltpu.VMEM),) * 5,
        scratch_shapes=[
            vm(q.shape, BF), vm(g.shape, BF), vm(proj.shape, BF), vm((rank, TOK), BF), vm(weight.shape, BF),
            pltpu.SMEM(lengths.shape, jnp.int32),
            vm((win, HEAD), BF), vm((win, HEAD), BF), vm((HEAD, win), BF),
            vm((PER, SPAN * BLOCK, ROWS), F32), vm((PER, SPAN * BLOCK, ROWS), F32),
            vm((PER, SPAN * BLOCK, ROWS), BF), vm((PER, SPAN * BLOCK, ROWS), BF),
            vm((PER, 8, ROWS), F32),
            vm((REACH + 1, 2, TOK, HEAD), F32), vm((4, 2, TOK, HEAD), BF), vm((5, 2, TOK, HEAD), BF),
            vm((rank, TOK), F32), vm((PER, rank, BLOCK), BF), vm((PER, zs, rank, BLOCK), BF),
            vm((rank, feats), F32), vm((rank, wide), F32), vm((rank, feats), BF), vm((rank, wide), BF),
            vm((n_a, 16, feats // NCORE), BF), vm((n_a, 16, wide // NCORE), BF),
            vm((n_y, 16, feats // NCORE), BF), vm((n_y, 16, wide // NCORE), BF),
            vm((rank, feats), BF), vm((rank, wide), BF),
            dma((8,)), dma((5, 2)), dma((REACH, 2)), dma((4,)), dma((5,)),
            dma((PER, zs)), dma((PER, zs)), dma((2, n_a)), dma((2, n_a)), dma((2, ys)), dma((2, ys)),
            dma((2, n_a)), dma((2, n_a)),
        ],
        compiler_params=pltpu.CompilerParams(
            collective_id=0, has_side_effects=True, vmem_limit_bytes=56 * 2**20
        ),
        cost_estimate=pl.CostEstimate(flops=3_200_000_000, bytes_accessed=4_000_000, transcendentals=2_400_000),
        name="attention_backward",
    )(q, k, v, g, proj, hidden.T, weight, lengths)
    qg, dk, dv, down, up = pl.pallas_call(
        hand_over,
        out_shape=tuple(jax.ShapeDtypeStruct(o.shape, o.dtype) for o in outs),
        in_specs=[pl.BlockSpec(memory_space=pltpu.VMEM)] * 5,
        out_specs=(anywhere,) * 5,
        scratch_shapes=[dma((5,))],
        compiler_params=pltpu.CompilerParams(vmem_limit_bytes=8 * 2**20),
        name="hand_over",
    )(*outs)
    return qg, dk, dv, down.T, up


def solution(mesh):
    n_ctx, n_kvh = mesh.shape["ctx"], mesh.shape["kvh"]
    both = P("ctx", "kvh")
    return jax.shard_map(
        functools.partial(shards, n_ctx, n_kvh),
        mesh=mesh,
        in_specs=(both, both, both, both, both, P("ctx", None), P(None, "kvh"), P()),
        out_specs=(both, both, both, P("kvh", None), P(None, "kvh")),
        check_vma=False,
    )
```

```python
import functools
import math

import jax
import jax.numpy as jnp
from jax import lax
from jax.experimental import pallas as pl
from jax.experimental.pallas import tpu as pltpu
from jax.sharding import PartitionSpec as P

MESH = pl.DeviceIdType.MESH
HEAD = 128
HEADS = 4
BLOCK = 128
REACH = 4
TOK = 384
PER = TOK // BLOCK
SPAN = 12
ROWS = HEADS * BLOCK
NX, NCORE = 4, 2
FAR = 1e30
BF = jnp.bfloat16
F32 = jnp.float32

NT = (((1,), (1,)), ((), ()))
NN = (((1,), (0,)), ((), ()))


def dot(a, b, dims=NN):
    return lax.dot_general(a, b, dims, preferred_element_type=F32)


def fold8(tile, op):
    parts = tile.reshape(tile.shape[0] // 8, 8, tile.shape[1])
    return op(parts, axis=0)


def by_distance(n):
    return sorted(range(1, n), key=lambda o: -min(o, n - o))


def kernel(
    n_ctx, n_kvh, q_hbm, k_hbm, v_hbm, g_hbm, x_hbm, a_hbm, w_hbm, len_hbm,
    qg_ref, dk_ref, dv_ref, down_out, up_out,
    q_ref, g_ref, x_ref, a_ref, w_ref, len_ref, kwin, vwin, kwin_t, s_ref, dp_ref, p_ref, ds_ref,
    top_ref, level_ref, sum_ref, near, back, got,
    mix_own, mix_send, mix_got,
    down_own, up_own, down_send, up_send, down_a, up_a, down_y, up_y, down_fin, up_fin,
    in_sem, halo_s, halo_r, back_s, back_r, mix_s, mix_r, rs_s, rs_r, ys_s, ys_r, ag_s, ag_r,
):
    n_y = n_ctx // (NX * NCORE)
    c = lax.axis_index("ctx")
    z = lax.axis_index("kvh")
    core = lax.rem(c, NCORE)
    x = lax.rem(c // NCORE, NX)
    y = c // (NX * NCORE)

    def at(yy, xx, cc):
        return ((yy * NX + xx) * NCORE + cc, z)

    def along(d):
        return (lax.rem(c + d + n_ctx, n_ctx), z)

    z_peers = [s + (s >= z).astype(jnp.int32) for s in range(n_kvh - 1)]
    y_peers = [lax.rem(y + o, n_y) for o in by_distance(n_y)]
    a_peers = [
        (lax.rem(x + dx, NX), lax.rem(core + dc, NCORE)) for dx in by_distance(NX) for dc in range(NCORE)
    ] + [(x, 1 - core)]

    own = pl.ds(REACH * TOK, TOK)
    local = [
        pltpu.make_async_copy(src, dst, in_sem.at[i])
        for i, (src, dst) in enumerate([
            (q_hbm, q_ref), (k_hbm, kwin.at[own]), (g_hbm, g_ref), (v_hbm, vwin.at[own]),
            (len_hbm, len_ref), (w_hbm, w_ref), (a_hbm, a_ref), (x_hbm, x_ref),
        ])
    ]
    lq, lk, lg, lv, llen, lw, la, lx = local

    barrier = pltpu.get_barrier_semaphore()
    greet = [along(d) for d in (1, 3, 4, -1, -3, -4)]
    greet += [(c, zz) for zz in z_peers]
    greet += [at(yy, x, core) for yy in y_peers]
    greet += [at(y, xx, cc) for xx, cc in a_peers]
    for who in greet:
        pl.semaphore_signal(barrier, inc=1, device_id=who, device_id_type=MESH)
    for cp in local:
        cp.start()
    pl.semaphore_wait(barrier, len(greet))

    mate = along(1 - 2 * core)
    first_core, second_core = core == 0, core == 1

    def slot_rows(d, first=0):
        return pl.ds((REACH - d) * TOK + first, TOK - first)

    def forward(n, j, src, d, to, first=0):
        return pltpu.make_async_remote_copy(
            src_ref=src, dst_ref=(kwin, vwin)[j].at[slot_rows(d, first)],
            send_sem=halo_s.at[n, j], recv_sem=halo_r.at[d - 1, j], device_id=to, device_id_type=MESH,
        )

    def held(j, d, first=0):
        return (kwin, vwin)[j].at[slot_rows(d, first)]

    def own_to(j, d):
        first = BLOCK if d == REACH else 0
        return forward(max(d - 2, 0), j, (k_hbm, v_hbm)[j].at[pl.ds(first, TOK - first)], d, along(d), first)

    def pass_mate(j, d):
        return forward(3, j, held(j, d), 2, mate)

    def pass_last(j):
        return forward(4, j, held(j, 3, BLOCK), REACH, mate, BLOCK)

    def arrived(j, d):
        first = BLOCK if d == REACH else 0
        forward(0, j, held(j, d, first), d, along(1), first).wait_recv()

    @pl.when(first_core)
    def _():
        for d, j in ((3, 0), (1, 0), (3, 1), (1, 1), (4, 0), (4, 1)):
            own_to(j, d).start()

    @pl.when(second_core)
    def _():
        for d, j in ((1, 0), (1, 1), (3, 0), (3, 1)):
            own_to(j, d).start()

    llen.wait()
    firsts = [jnp.int32(0)] * PER
    start = jnp.int32(0)
    for doc in range(len_hbm.shape[0]):
        for i in range(PER):
            firsts[i] = jnp.where(start <= c * PER + i, start, firsts[i])
        start = start + len_ref[doc]

    def away(i, slot):
        block = c * PER + i + slot - (SPAN - 1)
        return jnp.where(block >= firsts[i], 0.0, FAR).astype(F32)

    def rows_of(ref, i):
        return jnp.concatenate(
            [ref[i * BLOCK:(i + 1) * BLOCK, h * HEAD:(h + 1) * HEAD] for h in range(HEADS)], axis=0
        )

    for i in range(PER):
        top_ref[i] = jnp.full((8, ROWS), -2.0 * FAR, F32)

    causal = (
        lax.broadcasted_iota(jnp.int32, (BLOCK, ROWS), 0)
        <= lax.broadcasted_iota(jnp.int32, (BLOCK, ROWS), 1) % BLOCK
    )

    def window(d, i):
        low = (REACH - d) * PER
        return max(low, i + 1), min(low + PER, i + SPAN + 1)

    def scores(d):
        for i in range(PER):
            lo, hi = window(d, i)
            if lo >= hi:
                continue
            s = dot(kwin[lo * BLOCK:hi * BLOCK], rows_of(q_ref, i), NT)
            top = top_ref[i]
            for w in range(lo, hi):
                slot = w - i - 1
                tile = s[(w - lo) * BLOCK:(w - lo + 1) * BLOCK]
                if slot == SPAN - 1:
                    tile = jnp.where(causal, tile, -FAR)
                s_ref[i, slot * BLOCK:(slot + 1) * BLOCK] = tile
                top = jnp.maximum(top, fold8(tile, jnp.max) - away(i, slot))
            top_ref[i] = top
        low = (REACH - d) * TOK + (BLOCK if d == REACH else 0)
        high = (REACH - d + 1) * TOK
        kwin_t[:, low:high] = kwin[low:high].T

    def dprobs(d):
        for i in range(PER):
            lo, hi = window(d, i)
            if lo >= hi:
                continue
            dp_ref[i, (lo - i - 1) * BLOCK:(hi - i - 1) * BLOCK] = dot(
                vwin[lo * BLOCK:hi * BLOCK], rows_of(g_ref, i), NT
            )

    factor = HEAD ** -0.5
    rate = factor * math.log2(math.e)
    STEP = 64
    zero = jnp.zeros((8, ROWS), F32)

    def weights(d):
        for i in range(PER):
            lo, hi = window(d, i)
            if lo >= hi:
                continue
            top = jnp.max(top_ref[i], axis=0, keepdims=True)
            level_ref[d, i] = jnp.broadcast_to(top, (8, ROWS))
            total, delta = zero, zero
            for w in range(lo, hi):
                slot = w - i - 1
                level = top + away(i, slot)

                def weigh(t, carry, i=i, slot=slot, level=level):
                    total, delta = carry
                    span = pl.ds(pl.multiple_of(slot * BLOCK + t * STEP, STEP), STEP)
                    p = jnp.exp2((s_ref[i, span] - level) * rate)
                    s_ref[i, span] = p
                    return total + fold8(p, jnp.sum), delta + fold8(p * dp_ref[i, span], jnp.sum)

                total, delta = lax.fori_loop(0, BLOCK // STEP, weigh, (total, delta), unroll=True)
            sum_ref[d, i, 0] = total
            sum_ref[d, i, 1] = delta

    def attend(d):
        scores(d)
        dprobs(d)
        weights(d)

    lq.wait()
    lk.wait()
    lg.wait()
    lv.wait()
    attend(0)

    @pl.when(second_core)
    def _():
        for j in range(2):
            arrived(j, 1)
        attend(1)
        for j in range(2):
            arrived(j, 3)
            pass_mate(j, 3).start()
        attend(3)

    @pl.when(first_core)
    def _():
        for j in range(2):
            arrived(j, 1)
            pass_mate(j, 1).start()
        attend(1)

    for j in range(2):
        arrived(j, 2)
    attend(2)

    @pl.when(first_core)
    def _():
        for j in range(2):
            arrived(j, 3)
            pass_last(j).start()
        attend(3)

    mix_copies = []

    def mix_copy(i, s):
        slot = z - (z > z_peers[s]).astype(jnp.int32)
        return pltpu.make_async_remote_copy(
            src_ref=mix_send.at[i], dst_ref=mix_got.at[i, slot],
            send_sem=mix_s.at[i, s], recv_sem=mix_r.at[i, slot],
            device_id=(c, z_peers[s]), device_id_type=MESH,
        )

    def mix_arrived(i, s):
        pltpu.make_async_remote_copy(
            src_ref=mix_send.at[i], dst_ref=mix_got.at[i, s],
            send_sem=mix_s.at[i, s], recv_sem=mix_r.at[i, s],
            device_id=(c, z_peers[s]), device_id_type=MESH,
        ).wait_recv()

    def finish(i):
        top = jnp.max(top_ref[i], axis=0, keepdims=True)
        near_ranges = [d for d in range(REACH + 1) if window(d, i)[0] < window(d, i)[1]]
        fades = {d: jnp.exp2((level_ref[d, i, :1] - top) * rate) for d in near_ranges}
        total, delta = zero, zero
        for d in near_ranges:
            total = total + sum_ref[d, i, 0] * fades[d]
            delta = delta + sum_ref[d, i, 1] * fades[d]
        share = 1.0 / jnp.sum(total, axis=0, keepdims=True)
        delta = jnp.sum(delta, axis=0, keepdims=True) * share
        for d in near_ranges:
            lo, hi = window(d, i)
            start = (lo - i - 1) * BLOCK
            part = fades[d] * share
            level_ref[d, i] = jnp.broadcast_to(part, (8, ROWS))

            def settle(t, carry, i=i, start=start, part=part, delta=delta):
                span = pl.ds(pl.multiple_of(start + t * STEP, STEP), STEP)
                p = s_ref[i, span] * part
                ds_ref[i, span] = (p * (dp_ref[i, span] - delta)).astype(BF)
                return carry

            lax.fori_loop(0, (hi - lo) * BLOCK // STEP, settle, 0)
        dq = dot(kwin_t[:, (i + 1) * BLOCK:(i + 1 + SPAN) * BLOCK], ds_ref[i]) * factor
        for h in range(HEADS):
            qg_ref[i * BLOCK:(i + 1) * BLOCK, h * HEAD:(h + 1) * HEAD] = (
                dq[:, h * HEAD:(h + 1) * HEAD].T.astype(BF)
            )
        mixed = dot(w_ref[...], qg_ref[i * BLOCK:(i + 1) * BLOCK], NT)
        mix_own[:, i * BLOCK:(i + 1) * BLOCK] = mixed
        mix_send[i] = mixed.astype(BF)
        for n in range(n_kvh - 1):
            cp = mix_copy(i, n)
            cp.start()
            mix_copies.append(cp)

    lw.wait()
    finish(2)
    for j in range(2):
        arrived(j, REACH)
    attend(REACH)
    finish(1)
    finish(0)

    def chunk(ref, xx, cc):
        width = ref.shape[1] // NCORE
        return ref.at[pl.ds(pl.multiple_of(xx * 16, 16), 16), pl.ds(pl.multiple_of(cc * width, 128), width)]

    def scatter(which, send, got):
        copies = []
        for o, (xx, cc) in enumerate(a_peers):
            cp = pltpu.make_async_remote_copy(
                src_ref=chunk(send, xx, cc), dst_ref=got.at[o],
                send_sem=rs_s.at[which, o], recv_sem=rs_r.at[which, o],
                device_id=at(y, xx, cc), device_id_type=MESH,
            )
            cp.start()
            copies.append(cp)
        return copies

    def exchange(which, copies, own_part, got, slots):
        for cp in copies:
            cp.wait_recv()
        part = chunk(own_part, x, core)[...]
        for o in range(len(a_peers)):
            part = part + got[o].astype(F32)
        slots[y] = part.astype(BF)
        out = []
        for o, yy in enumerate(y_peers):
            cp = pltpu.make_async_remote_copy(
                src_ref=slots.at[y], dst_ref=slots.at[y],
                send_sem=ys_s.at[which, o], recv_sem=ys_r.at[which, o],
                device_id=at(yy, x, core), device_id_type=MESH,
            )
            cp.start()
            out.append(cp)
        return out

    def gather(which, copies, slots, fin):
        for cp in copies:
            cp.wait_recv()
        part = slots[0].astype(F32)
        for yy in range(1, n_y):
            part = part + slots[yy].astype(F32)
        mine = chunk(fin, x, core)
        mine[...] = part.astype(BF)
        out = []
        for o, (xx, cc) in enumerate(a_peers):
            cp = pltpu.make_async_remote_copy(
                src_ref=mine, dst_ref=mine,
                send_sem=ag_s.at[which, o], recv_sem=ag_r.at[which, o],
                device_id=at(y, xx, cc), device_id_type=MESH,
            )
            cp.start()
            out.append(cp)
        return out

    la.wait()
    up = dot(a_ref[...], qg_ref[...])
    up_own[...] = up
    up_send[...] = up.astype(BF)
    up_rs = scatter(0, up_send, up_a)

    def ranges(d):
        for i in range(PER):
            lo, hi = window(d, i)
            if lo >= hi:
                continue
            start = (lo - i - 1) * BLOCK
            part = level_ref[d, i, :1]

            def normal(t, carry, i=i, start=start, part=part):
                span = pl.ds(pl.multiple_of(start + t * STEP, STEP), STEP)
                p_ref[i, span] = (s_ref[i, span] * part).astype(BF)
                return carry

            lax.fori_loop(0, (hi - lo) * BLOCK // STEP, normal, 0)
        low = (REACH - d) * PER
        dk = jnp.zeros((TOK, HEAD), F32)
        dv = jnp.zeros((TOK, HEAD), F32)
        parts_k, parts_v = [None] * PER, [None] * PER
        for i in range(PER):
            lo, hi = window(d, i)
            if lo >= hi:
                continue
            span = slice((lo - i - 1) * BLOCK, (hi - i - 1) * BLOCK)
            k_part = dot(ds_ref[i, span], rows_of(q_ref, i))
            v_part = dot(p_ref[i, span], rows_of(g_ref, i))
            for w in range(lo, hi):
                at_w = slice((w - lo) * BLOCK, (w - lo + 1) * BLOCK)
                b = w - low
                parts_k[b] = k_part[at_w] if parts_k[b] is None else parts_k[b] + k_part[at_w]
                parts_v[b] = v_part[at_w] if parts_v[b] is None else parts_v[b] + v_part[at_w]
        return parts_k, parts_v

    def store(d):
        parts = ranges(d)
        first = BLOCK if d == REACH else 0
        for j in range(2):
            for b in range(first // BLOCK, PER):
                value = parts[j][b] * factor if j == 0 else parts[j][b]
                near[d, j, b * BLOCK:(b + 1) * BLOCK] = value.astype(near.dtype)

    def send_back(n, src, slot, to, first=0):
        rows = pl.ds(first, TOK - first)
        return pltpu.make_async_remote_copy(
            src_ref=src.at[:, rows], dst_ref=got.at[slot, :, rows],
            send_sem=back_s.at[n], recv_sem=back_r.at[slot], device_id=to, device_id_type=MESH,
        )

    def came_back(slot, first=0):
        send_back(0, got.at[slot], slot, along(-1), first).wait_recv()

    back_4 = send_back(0, back.at[0], 0, along(-1), BLOCK)
    back_2 = send_back(1, back.at[1], 1, mate)
    back_1 = send_back(2, back.at[2], 2, along(-1))
    back_3 = send_back(2, back.at[2], 3, along(-2))
    last_0 = send_back(3, back.at[3], 4, along(-1))
    last_1 = send_back(3, back.at[3], 4, along(-3))

    store(REACH)
    back[0, :, BLOCK:] = near[REACH, :, BLOCK:].astype(BF)
    back_4.start()
    store(2)
    back[1] = near[2].astype(BF)
    back_2.start()
    store(1)
    store(3)

    @pl.when(second_core)
    def _():
        back[2] = near[1].astype(BF)
        back_1.start()

    @pl.when(first_core)
    def _():
        came_back(0, BLOCK)
        back[2, :, :BLOCK] = near[3, :, :BLOCK].astype(BF)
        back[2, :, BLOCK:] = (near[3, :, BLOCK:] + got[0, :, BLOCK:].astype(F32)).astype(BF)
        back_3.start()

    store(0)

    lx.wait()
    for i in range(PER - 1, -1, -1):
        cols = slice(i * BLOCK, (i + 1) * BLOCK)
        mixed = mix_own[:, cols]
        for n in range(n_kvh - 1):
            mix_arrived(i, n)
            mixed = mixed + mix_got[i, n].astype(F32)
        part = dot(mixed.astype(BF), x_ref[cols])
        if i < PER - 1:
            part = part + down_own[...]
        down_own[...] = part
        if i == 0:
            down_send[...] = part.astype(BF)
    down_rs = scatter(1, down_send, down_a)
    up_ys = exchange(0, up_rs, up_own, up_a, up_y)
    down_ys = exchange(1, down_rs, down_own, down_a, down_y)
    up_ag = gather(0, up_ys, up_y, up_fin)

    came_back(1)

    @pl.when(first_core)
    def _():
        came_back(3)
        back[3] = (near[1] + got[1].astype(F32) + got[3].astype(F32)).astype(BF)
        last_0.start()

    @pl.when(second_core)
    def _():
        came_back(0, BLOCK)
        back[3, :, :BLOCK] = (near[3, :, :BLOCK] + got[1, :, :BLOCK].astype(F32)).astype(BF)
        back[3, :, BLOCK:] = (
            near[3, :, BLOCK:] + got[1, :, BLOCK:].astype(F32) + got[0, :, BLOCK:].astype(F32)
        ).astype(BF)
        last_1.start()

    down_ag = gather(1, down_ys, down_y, down_fin)

    @pl.when(first_core)
    def _():
        came_back(2)
        near[0] = near[0] + got[2].astype(F32)

    came_back(4)
    dk_ref[...] = (near[0, 0] + got[4, 0].astype(F32)).astype(BF)
    dv_ref[...] = (near[0, 1] + got[4, 1].astype(F32)).astype(BF)

    scale = (TOK * n_ctx) ** -0.5
    for cp in up_ag:
        cp.wait_recv()
    up_out[...] = up_fin[...].astype(F32) * scale
    for cp in down_ag:
        cp.wait_recv()
    down_out[...] = down_fin[...].astype(F32) * scale

    @pl.when(first_core)
    def _():
        for j in range(2):
            own_to(j, REACH).wait_send()
            pass_mate(j, 1).wait_send()
            pass_last(j).wait_send()
        back_3.wait_send()
        last_0.wait_send()

    @pl.when(second_core)
    def _():
        for j in range(2):
            pass_mate(j, 3).wait_send()
        back_1.wait_send()
        last_1.wait_send()

    for j in range(2):
        own_to(j, 1).wait_send()
        own_to(j, 3).wait_send()
    back_4.wait_send()
    back_2.wait_send()
    for group in (mix_copies, up_rs, down_rs, up_ys, down_ys, up_ag, down_ag):
        for cp in group:
            cp.wait_send()


def hand_over(*refs):
    arrays, results, sem = refs[:5], refs[5:10], refs[10]
    out = [pltpu.make_async_copy(arrays[i], results[i], sem.at[i]) for i in range(5)]
    for cp in out:
        cp.start()
    for cp in out:
        cp.wait()


def shards(n_ctx, n_kvh, q, k, v, g, proj, hidden, weight, lengths):
    n_y = n_ctx // (NX * NCORE)
    n_a = NX * NCORE - 1
    feats, rank = proj.shape[1], hidden.shape[1]
    wide = q.shape[1]
    vm = pltpu.VMEM
    dma = pltpu.SemaphoreType.DMA
    win = (REACH + 1) * TOK
    anywhere = pl.BlockSpec(memory_space=pl.ANY)
    zs, ys = max(n_kvh - 1, 1), max(n_y - 1, 1)
    outs = pl.pallas_call(
        functools.partial(kernel, n_ctx, n_kvh),
        out_shape=(
            pltpu.VMEM(q.shape, BF),
            pltpu.VMEM(k.shape, BF),
            pltpu.VMEM(v.shape, BF),
            pltpu.VMEM((rank, feats), F32),
            pltpu.VMEM((rank, wide), F32),
        ),
        in_specs=[anywhere] * 8,
        out_specs=(pl.BlockSpec(memory_space=pltpu.VMEM),) * 5,
        scratch_shapes=[
            vm(q.shape, BF), vm(g.shape, BF), vm(proj.shape, BF), vm((rank, TOK), BF), vm(weight.shape, BF),
            pltpu.SMEM(lengths.shape, jnp.int32),
            vm((win, HEAD), BF), vm((win, HEAD), BF), vm((HEAD, win), BF),
            vm((PER, SPAN * BLOCK, ROWS), F32), vm((PER, SPAN * BLOCK, ROWS), F32),
            vm((PER, SPAN * BLOCK, ROWS), BF), vm((PER, SPAN * BLOCK, ROWS), BF),
            vm((PER, 8, ROWS), F32), vm((REACH + 1, PER, 8, ROWS), F32), vm((REACH + 1, PER, 2, 8, ROWS), F32),
            vm((REACH + 1, 2, TOK, HEAD), F32), vm((4, 2, TOK, HEAD), BF), vm((5, 2, TOK, HEAD), BF),
            vm((rank, TOK), F32), vm((PER, rank, BLOCK), BF), vm((PER, zs, rank, BLOCK), BF),
            vm((rank, feats), F32), vm((rank, wide), F32), vm((rank, feats), BF), vm((rank, wide), BF),
            vm((n_a, 16, feats // NCORE), BF), vm((n_a, 16, wide // NCORE), BF),
            vm((n_y, 16, feats // NCORE), BF), vm((n_y, 16, wide // NCORE), BF),
            vm((rank, feats), BF), vm((rank, wide), BF),
            dma((8,)), dma((5, 2)), dma((REACH, 2)), dma((4,)), dma((5,)),
            dma((PER, zs)), dma((PER, zs)), dma((2, n_a)), dma((2, n_a)), dma((2, ys)), dma((2, ys)),
            dma((2, n_a)), dma((2, n_a)),
        ],
        compiler_params=pltpu.CompilerParams(
            collective_id=0, has_side_effects=True, vmem_limit_bytes=56 * 2**20
        ),
        cost_estimate=pl.CostEstimate(flops=3_200_000_000, bytes_accessed=4_000_000, transcendentals=2_400_000),
        name="attention_backward",
    )(q, k, v, g, proj, hidden.T, weight, lengths)
    qg, dk, dv, down, up = pl.pallas_call(
        hand_over,
        out_shape=tuple(jax.ShapeDtypeStruct(o.shape, o.dtype) for o in outs),
        in_specs=[pl.BlockSpec(memory_space=pltpu.VMEM)] * 5,
        out_specs=(anywhere,) * 5,
        scratch_shapes=[dma((5,))],
        compiler_params=pltpu.CompilerParams(vmem_limit_bytes=8 * 2**20),
        name="hand_over",
    )(*outs)
    return qg, dk, dv, down.T, up


def solution(mesh):
    n_ctx, n_kvh = mesh.shape["ctx"], mesh.shape["kvh"]
    both = P("ctx", "kvh")
    return jax.shard_map(
        functools.partial(shards, n_ctx, n_kvh),
        mesh=mesh,
        in_specs=(both, both, both, both, both, P("ctx", None), P(None, "kvh"), P()),
        out_specs=(both, both, both, P("kvh", None), P(None, "kvh")),
        check_vma=False,
    )
```

```python
import functools
import math

import jax
import jax.numpy as jnp
from jax import lax
from jax.experimental import pallas as pl
from jax.experimental.pallas import tpu as pltpu
from jax.sharding import PartitionSpec as P

MESH = pl.DeviceIdType.MESH
HEAD = 128
HEADS = 4
BLOCK = 128
REACH = 4
TOK = 384
PER = TOK // BLOCK
SPAN = 12
ROWS = HEADS * BLOCK
NX, NCORE = 4, 2
FAR = 1e30
BF = jnp.bfloat16
F32 = jnp.float32

NT = (((1,), (1,)), ((), ()))
NN = (((1,), (0,)), ((), ()))


def dot(a, b, dims=NN):
    return lax.dot_general(a, b, dims, preferred_element_type=F32)


def fold8(tile, op):
    parts = tile.reshape(tile.shape[0] // 8, 8, tile.shape[1])
    return op(parts, axis=0)


def by_distance(n):
    return sorted(range(1, n), key=lambda o: -min(o, n - o))


def kernel(
    n_ctx, n_kvh, q_hbm, k_hbm, v_hbm, g_hbm, x_hbm, a_hbm, w_hbm, len_hbm,
    qg_ref, dk_ref, dv_ref, down_out, up_out,
    q_ref, g_ref, x_ref, a_ref, w_ref, len_ref, kwin, vwin, relay, kwin_t, s_ref, dp_ref, p_ref, ds_ref,
    top_ref, level_ref, sum_ref, near, back, got,
    mix_own, mix_send, mix_got,
    down_own, up_own, down_send, up_send, down_a, up_a, down_y, up_y, down_fin, up_fin,
    in_sem, halo_s, halo_r, back_s, back_r, mix_s, mix_r, rs_s, rs_r, ys_s, ys_r, ag_s, ag_r,
):
    n_y = n_ctx // (NX * NCORE)
    c = lax.axis_index("ctx")
    z = lax.axis_index("kvh")
    core = lax.rem(c, NCORE)
    x = lax.rem(c // NCORE, NX)
    y = c // (NX * NCORE)

    def at(yy, xx, cc):
        return ((yy * NX + xx) * NCORE + cc, z)

    def along(d):
        return (lax.rem(c + d + n_ctx, n_ctx), z)

    z_peers = [s + (s >= z).astype(jnp.int32) for s in range(n_kvh - 1)]
    y_peers = [lax.rem(y + o, n_y) for o in by_distance(n_y)]
    a_peers = [
        (lax.rem(x + dx, NX), lax.rem(core + dc, NCORE)) for dx in by_distance(NX) for dc in range(NCORE)
    ] + [(x, 1 - core)]

    own = pl.ds(REACH * TOK, TOK)
    local = [
        pltpu.make_async_copy(src, dst, in_sem.at[i])
        for i, (src, dst) in enumerate([
            (q_hbm, q_ref), (k_hbm, kwin.at[own]), (g_hbm, g_ref), (v_hbm, vwin.at[own]),
            (len_hbm, len_ref), (w_hbm, w_ref), (a_hbm, a_ref), (x_hbm, x_ref),
        ])
    ]
    lq, lk, lg, lv, llen, lw, la, lx = local

    barrier = pltpu.get_barrier_semaphore()
    greet = [along(d) for d in (1, 3, 6, -1, -3, -6)]
    greet += [(c, zz) for zz in z_peers]
    greet += [at(yy, x, core) for yy in y_peers]
    greet += [at(y, xx, cc) for xx, cc in a_peers]
    for who in greet:
        pl.semaphore_signal(barrier, inc=1, device_id=who, device_id_type=MESH)
    for cp in local:
        cp.start()
    pl.semaphore_wait(barrier, len(greet))

    mate = along(1 - 2 * core)
    first_core, second_core = core == 0, core == 1

    def slot_rows(d, first=0):
        return pl.ds((REACH - d) * TOK + first, TOK - first)

    def forward(n, j, src, d, to, first=0):
        return pltpu.make_async_remote_copy(
            src_ref=src, dst_ref=(kwin, vwin)[j].at[slot_rows(d, first)],
            send_sem=halo_s.at[n, j], recv_sem=halo_r.at[d - 1, j], device_id=to, device_id_type=MESH,
        )

    def held(j, d, first=0):
        return (kwin, vwin)[j].at[slot_rows(d, first)]

    def own_to(j, d):
        return forward(d // 2, j, (k_hbm, v_hbm)[j], d, along(d))

    def own_round(j):
        return pltpu.make_async_remote_copy(
            src_ref=(k_hbm, v_hbm)[j].at[pl.ds(BLOCK, TOK - BLOCK)], dst_ref=relay.at[j],
            send_sem=halo_s.at[2, j], recv_sem=halo_r.at[REACH, j],
            device_id=at(y, lax.rem(x + NX - 1, NX), core), device_id_type=MESH,
        )

    def pass_round(j):
        to = along(jnp.where(x == NX - 1, -2, 6))
        return forward(5, j, relay.at[j], REACH, to, BLOCK)

    def pass_mate(j, d):
        return forward(3, j, held(j, d), 2, mate)

    def pass_last(j):
        return forward(4, j, held(j, 3, BLOCK), REACH, mate, BLOCK)

    def arrived(j, d):
        first = BLOCK if d == REACH else 0
        forward(0, j, held(j, d, first), d, along(1), first).wait_recv()

    @pl.when(first_core)
    def _():
        for d, j in ((3, 0), (1, 0), (3, 1), (1, 1)):
            own_to(j, d).start()
            if d == 3:
                own_round(j).start()

    @pl.when(second_core)
    def _():
        for d, j in ((1, 0), (1, 1), (3, 0), (3, 1)):
            own_to(j, d).start()

    llen.wait()
    firsts = [jnp.int32(0)] * PER
    start = jnp.int32(0)
    for doc in range(len_hbm.shape[0]):
        for i in range(PER):
            firsts[i] = jnp.where(start <= c * PER + i, start, firsts[i])
        start = start + len_ref[doc]

    def away(i, slot):
        block = c * PER + i + slot - (SPAN - 1)
        return jnp.where(block >= firsts[i], 0.0, FAR).astype(F32)

    def rows_of(ref, i):
        return jnp.concatenate(
            [ref[i * BLOCK:(i + 1) * BLOCK, h * HEAD:(h + 1) * HEAD] for h in range(HEADS)], axis=0
        )

    for i in range(PER):
        top_ref[i] = jnp.full((8, ROWS), -2.0 * FAR, F32)

    causal = (
        lax.broadcasted_iota(jnp.int32, (BLOCK, ROWS), 0)
        <= lax.broadcasted_iota(jnp.int32, (BLOCK, ROWS), 1) % BLOCK
    )

    def window(d, i):
        low = (REACH - d) * PER
        return max(low, i + 1), min(low + PER, i + SPAN + 1)

    def scores(d):
        for i in range(PER):
            lo, hi = window(d, i)
            if lo >= hi:
                continue
            s = dot(kwin[lo * BLOCK:hi * BLOCK], rows_of(q_ref, i), NT)
            top = top_ref[i]
            for w in range(lo, hi):
                slot = w - i - 1
                tile = s[(w - lo) * BLOCK:(w - lo + 1) * BLOCK]
                if slot == SPAN - 1:
                    tile = jnp.where(causal, tile, -FAR)
                s_ref[i, slot * BLOCK:(slot + 1) * BLOCK] = tile
                top = jnp.maximum(top, fold8(tile, jnp.max) - away(i, slot))
            top_ref[i] = top
        low = (REACH - d) * TOK + (BLOCK if d == REACH else 0)
        high = (REACH - d + 1) * TOK
        kwin_t[:, low:high] = kwin[low:high].T

    def dprobs(d):
        for i in range(PER):
            lo, hi = window(d, i)
            if lo >= hi:
                continue
            dp_ref[i, (lo - i - 1) * BLOCK:(hi - i - 1) * BLOCK] = dot(
                vwin[lo * BLOCK:hi * BLOCK], rows_of(g_ref, i), NT
            )

    factor = HEAD ** -0.5
    rate = factor * math.log2(math.e)
    STEP = 64
    zero = jnp.zeros((8, ROWS), F32)

    def weights(d):
        for i in range(PER):
            lo, hi = window(d, i)
            if lo >= hi:
                continue
            top = jnp.max(top_ref[i], axis=0, keepdims=True)
            level_ref[d, i] = jnp.broadcast_to(top, (8, ROWS))
            total, delta = zero, zero
            for w in range(lo, hi):
                slot = w - i - 1
                level = top + away(i, slot)

                def weigh(t, carry, i=i, slot=slot, level=level):
                    total, delta = carry
                    span = pl.ds(pl.multiple_of(slot * BLOCK + t * STEP, STEP), STEP)
                    p = jnp.exp2((s_ref[i, span] - level) * rate)
                    s_ref[i, span] = p
                    return total + fold8(p, jnp.sum), delta + fold8(p * dp_ref[i, span], jnp.sum)

                total, delta = lax.fori_loop(0, BLOCK // STEP, weigh, (total, delta), unroll=True)
            sum_ref[d, i, 0] = total
            sum_ref[d, i, 1] = delta

    def attend(d):
        scores(d)
        dprobs(d)
        weights(d)

    lq.wait()
    lk.wait()
    lg.wait()
    lv.wait()
    attend(0)

    @pl.when(second_core)
    def _():
        for j in range(2):
            arrived(j, 1)
        attend(1)
        for j in range(2):
            arrived(j, 3)
            pass_mate(j, 3).start()
        attend(3)

    @pl.when(first_core)
    def _():
        for j in range(2):
            arrived(j, 1)
            pass_mate(j, 1).start()
        for j in range(2):
            own_round(j).wait_recv()
            pass_round(j).start()
        attend(1)

    for j in range(2):
        arrived(j, 2)
    attend(2)

    @pl.when(first_core)
    def _():
        for j in range(2):
            arrived(j, 3)
            pass_last(j).start()
        attend(3)

    mix_copies = []

    def mix_copy(i, s):
        slot = z - (z > z_peers[s]).astype(jnp.int32)
        return pltpu.make_async_remote_copy(
            src_ref=mix_send.at[i], dst_ref=mix_got.at[i, slot],
            send_sem=mix_s.at[i, s], recv_sem=mix_r.at[i, slot],
            device_id=(c, z_peers[s]), device_id_type=MESH,
        )

    def mix_arrived(i, s):
        pltpu.make_async_remote_copy(
            src_ref=mix_send.at[i], dst_ref=mix_got.at[i, s],
            send_sem=mix_s.at[i, s], recv_sem=mix_r.at[i, s],
            device_id=(c, z_peers[s]), device_id_type=MESH,
        ).wait_recv()

    def finish(i):
        top = jnp.max(top_ref[i], axis=0, keepdims=True)
        near_ranges = [d for d in range(REACH + 1) if window(d, i)[0] < window(d, i)[1]]
        fades = {d: jnp.exp2((level_ref[d, i, :1] - top) * rate) for d in near_ranges}
        total, delta = zero, zero
        for d in near_ranges:
            total = total + sum_ref[d, i, 0] * fades[d]
            delta = delta + sum_ref[d, i, 1] * fades[d]
        share = 1.0 / jnp.sum(total, axis=0, keepdims=True)
        delta = jnp.sum(delta, axis=0, keepdims=True) * share
        for d in near_ranges:
            lo, hi = window(d, i)
            start = (lo - i - 1) * BLOCK
            part = fades[d] * share
            level_ref[d, i] = jnp.broadcast_to(part, (8, ROWS))

            def settle(t, carry, i=i, start=start, part=part, delta=delta):
                span = pl.ds(pl.multiple_of(start + t * STEP, STEP), STEP)
                p = s_ref[i, span] * part
                ds_ref[i, span] = (p * (dp_ref[i, span] - delta)).astype(BF)
                return carry

            lax.fori_loop(0, (hi - lo) * BLOCK // STEP, settle, 0)
        dq = dot(kwin_t[:, (i + 1) * BLOCK:(i + 1 + SPAN) * BLOCK], ds_ref[i]) * factor
        for h in range(HEADS):
            qg_ref[i * BLOCK:(i + 1) * BLOCK, h * HEAD:(h + 1) * HEAD] = (
                dq[:, h * HEAD:(h + 1) * HEAD].T.astype(BF)
            )
        mixed = dot(w_ref[...], qg_ref[i * BLOCK:(i + 1) * BLOCK], NT)
        mix_own[:, i * BLOCK:(i + 1) * BLOCK] = mixed
        mix_send[i] = mixed.astype(BF)
        for n in range(n_kvh - 1):
            cp = mix_copy(i, n)
            cp.start()
            mix_copies.append(cp)

    lw.wait()
    finish(2)
    for j in range(2):
        arrived(j, REACH)
    attend(REACH)
    finish(1)
    finish(0)

    def chunk(ref, xx, cc):
        width = ref.shape[1] // NCORE
        return ref.at[pl.ds(pl.multiple_of(xx * 16, 16), 16), pl.ds(pl.multiple_of(cc * width, 128), width)]

    def scatter(which, send, got):
        copies = []
        for o, (xx, cc) in enumerate(a_peers):
            cp = pltpu.make_async_remote_copy(
                src_ref=chunk(send, xx, cc), dst_ref=got.at[o],
                send_sem=rs_s.at[which, o], recv_sem=rs_r.at[which, o],
                device_id=at(y, xx, cc), device_id_type=MESH,
            )
            cp.start()
            copies.append(cp)
        return copies

    def exchange(which, copies, own_part, got, slots):
        for cp in copies:
            cp.wait_recv()
        part = chunk(own_part, x, core)[...]
        for o in range(len(a_peers)):
            part = part + got[o].astype(F32)
        slots[y] = part.astype(BF)
        out = []
        for o, yy in enumerate(y_peers):
            cp = pltpu.make_async_remote_copy(
                src_ref=slots.at[y], dst_ref=slots.at[y],
                send_sem=ys_s.at[which, o], recv_sem=ys_r.at[which, o],
                device_id=at(yy, x, core), device_id_type=MESH,
            )
            cp.start()
            out.append(cp)
        return out

    def gather(which, copies, slots, fin):
        for cp in copies:
            cp.wait_recv()
        part = slots[0].astype(F32)
        for yy in range(1, n_y):
            part = part + slots[yy].astype(F32)
        mine = chunk(fin, x, core)
        mine[...] = part.astype(BF)
        out = []
        for o, (xx, cc) in enumerate(a_peers):
            cp = pltpu.make_async_remote_copy(
                src_ref=mine, dst_ref=mine,
                send_sem=ag_s.at[which, o], recv_sem=ag_r.at[which, o],
                device_id=at(y, xx, cc), device_id_type=MESH,
            )
            cp.start()
            out.append(cp)
        return out

    la.wait()
    up = dot(a_ref[...], qg_ref[...])
    up_own[...] = up
    up_send[...] = up.astype(BF)
    up_rs = scatter(0, up_send, up_a)

    def ranges(d):
        for i in range(PER):
            lo, hi = window(d, i)
            if lo >= hi:
                continue
            start = (lo - i - 1) * BLOCK
            part = level_ref[d, i, :1]

            def normal(t, carry, i=i, start=start, part=part):
                span = pl.ds(pl.multiple_of(start + t * STEP, STEP), STEP)
                p_ref[i, span] = (s_ref[i, span] * part).astype(BF)
                return carry

            lax.fori_loop(0, (hi - lo) * BLOCK // STEP, normal, 0)
        low = (REACH - d) * PER
        dk = jnp.zeros((TOK, HEAD), F32)
        dv = jnp.zeros((TOK, HEAD), F32)
        parts_k, parts_v = [None] * PER, [None] * PER
        for i in range(PER):
            lo, hi = window(d, i)
            if lo >= hi:
                continue
            span = slice((lo - i - 1) * BLOCK, (hi - i - 1) * BLOCK)
            k_part = dot(ds_ref[i, span], rows_of(q_ref, i))
            v_part = dot(p_ref[i, span], rows_of(g_ref, i))
            for w in range(lo, hi):
                at_w = slice((w - lo) * BLOCK, (w - lo + 1) * BLOCK)
                b = w - low
                parts_k[b] = k_part[at_w] if parts_k[b] is None else parts_k[b] + k_part[at_w]
                parts_v[b] = v_part[at_w] if parts_v[b] is None else parts_v[b] + v_part[at_w]
        return parts_k, parts_v

    def store(d):
        parts = ranges(d)
        first = BLOCK if d == REACH else 0
        for j in range(2):
            for b in range(first // BLOCK, PER):
                value = parts[j][b] * factor if j == 0 else parts[j][b]
                near[d, j, b * BLOCK:(b + 1) * BLOCK] = value.astype(near.dtype)

    def send_back(n, src, slot, to, first=0):
        rows = pl.ds(first, TOK - first)
        return pltpu.make_async_remote_copy(
            src_ref=src.at[:, rows], dst_ref=got.at[slot, :, rows],
            send_sem=back_s.at[n], recv_sem=back_r.at[slot], device_id=to, device_id_type=MESH,
        )

    def came_back(slot, first=0):
        send_back(0, got.at[slot], slot, along(-1), first).wait_recv()

    back_4 = send_back(0, back.at[0], 0, along(-1), BLOCK)
    back_2 = send_back(1, back.at[1], 1, mate)
    back_1 = send_back(2, back.at[2], 2, along(-1))
    back_3 = send_back(2, back.at[2], 3, along(-2))
    last_0 = send_back(3, back.at[3], 4, along(-1))
    last_1 = send_back(3, back.at[3], 4, along(-3))

    store(REACH)
    back[0, :, BLOCK:] = near[REACH, :, BLOCK:].astype(BF)
    back_4.start()
    store(3)

    @pl.when(first_core)
    def _():
        came_back(0, BLOCK)
        back[2, :, :BLOCK] = near[3, :, :BLOCK].astype(BF)
        back[2, :, BLOCK:] = (near[3, :, BLOCK:] + got[0, :, BLOCK:].astype(F32)).astype(BF)
        back_3.start()

    store(2)
    back[1] = near[2].astype(BF)
    back_2.start()
    store(1)

    @pl.when(second_core)
    def _():
        back[2] = near[1].astype(BF)
        back_1.start()

    store(0)
    up_ys = exchange(0, up_rs, up_own, up_a, up_y)

    lx.wait()
    for i in range(PER - 1, -1, -1):
        cols = slice(i * BLOCK, (i + 1) * BLOCK)
        mixed = mix_own[:, cols]
        for n in range(n_kvh - 1):
            mix_arrived(i, n)
            mixed = mixed + mix_got[i, n].astype(F32)
        part = dot(mixed.astype(BF), x_ref[cols])
        if i < PER - 1:
            part = part + down_own[...]
        down_own[...] = part
        if i == 0:
            down_send[...] = part.astype(BF)
    down_rs = scatter(1, down_send, down_a)
    down_ys = exchange(1, down_rs, down_own, down_a, down_y)

    came_back(1)

    @pl.when(first_core)
    def _():
        came_back(3)
        back[3] = (near[1] + got[1].astype(F32) + got[3].astype(F32)).astype(BF)
        last_0.start()

    @pl.when(second_core)
    def _():
        came_back(0, BLOCK)
        back[3, :, :BLOCK] = (near[3, :, :BLOCK] + got[1, :, :BLOCK].astype(F32)).astype(BF)
        back[3, :, BLOCK:] = (
            near[3, :, BLOCK:] + got[1, :, BLOCK:].astype(F32) + got[0, :, BLOCK:].astype(F32)
        ).astype(BF)
        last_1.start()

    up_ag = gather(0, up_ys, up_y, up_fin)
    down_ag = gather(1, down_ys, down_y, down_fin)

    @pl.when(first_core)
    def _():
        came_back(2)
        near[0] = near[0] + got[2].astype(F32)

    came_back(4)
    dk_ref[...] = (near[0, 0] + got[4, 0].astype(F32)).astype(BF)
    dv_ref[...] = (near[0, 1] + got[4, 1].astype(F32)).astype(BF)

    scale = (TOK * n_ctx) ** -0.5
    for cp in up_ag:
        cp.wait_recv()
    up_out[...] = up_fin[...].astype(F32) * scale
    for cp in down_ag:
        cp.wait_recv()
    down_out[...] = down_fin[...].astype(F32) * scale

    @pl.when(first_core)
    def _():
        for j in range(2):
            own_round(j).wait_send()
            pass_round(j).wait_send()
            pass_mate(j, 1).wait_send()
            pass_last(j).wait_send()
        back_3.wait_send()
        last_0.wait_send()

    @pl.when(second_core)
    def _():
        for j in range(2):
            pass_mate(j, 3).wait_send()
        back_1.wait_send()
        last_1.wait_send()

    for j in range(2):
        own_to(j, 1).wait_send()
        own_to(j, 3).wait_send()
    back_4.wait_send()
    back_2.wait_send()
    for group in (mix_copies, up_rs, down_rs, up_ys, down_ys, up_ag, down_ag):
        for cp in group:
            cp.wait_send()


def hand_over(*refs):
    arrays, results, sem = refs[:5], refs[5:10], refs[10]
    out = [pltpu.make_async_copy(arrays[i], results[i], sem.at[i]) for i in range(5)]
    for cp in out:
        cp.start()
    for cp in out:
        cp.wait()


def shards(n_ctx, n_kvh, q, k, v, g, proj, hidden, weight, lengths):
    n_y = n_ctx // (NX * NCORE)
    n_a = NX * NCORE - 1
    feats, rank = proj.shape[1], hidden.shape[1]
    wide = q.shape[1]
    vm = pltpu.VMEM
    dma = pltpu.SemaphoreType.DMA
    win = (REACH + 1) * TOK
    anywhere = pl.BlockSpec(memory_space=pl.ANY)
    zs, ys = max(n_kvh - 1, 1), max(n_y - 1, 1)
    outs = pl.pallas_call(
        functools.partial(kernel, n_ctx, n_kvh),
        out_shape=(
            pltpu.VMEM(q.shape, BF),
            pltpu.VMEM(k.shape, BF),
            pltpu.VMEM(v.shape, BF),
            pltpu.VMEM((rank, feats), F32),
            pltpu.VMEM((rank, wide), F32),
        ),
        in_specs=[anywhere] * 8,
        out_specs=(pl.BlockSpec(memory_space=pltpu.VMEM),) * 5,
        scratch_shapes=[
            vm(q.shape, BF), vm(g.shape, BF), vm(proj.shape, BF), vm((rank, TOK), BF), vm(weight.shape, BF),
            pltpu.SMEM(lengths.shape, jnp.int32),
            vm((win, HEAD), BF), vm((win, HEAD), BF), vm((2, TOK - BLOCK, HEAD), BF), vm((HEAD, win), BF),
            vm((PER, SPAN * BLOCK, ROWS), F32), vm((PER, SPAN * BLOCK, ROWS), F32),
            vm((PER, SPAN * BLOCK, ROWS), BF), vm((PER, SPAN * BLOCK, ROWS), BF),
            vm((PER, 8, ROWS), F32), vm((REACH + 1, PER, 8, ROWS), F32), vm((REACH + 1, PER, 2, 8, ROWS), F32),
            vm((REACH + 1, 2, TOK, HEAD), F32), vm((4, 2, TOK, HEAD), BF), vm((5, 2, TOK, HEAD), BF),
            vm((rank, TOK), F32), vm((PER, rank, BLOCK), BF), vm((PER, zs, rank, BLOCK), BF),
            vm((rank, feats), F32), vm((rank, wide), F32), vm((rank, feats), BF), vm((rank, wide), BF),
            vm((n_a, 16, feats // NCORE), BF), vm((n_a, 16, wide // NCORE), BF),
            vm((n_y, 16, feats // NCORE), BF), vm((n_y, 16, wide // NCORE), BF),
            vm((rank, feats), BF), vm((rank, wide), BF),
            dma((8,)), dma((6, 2)), dma((REACH + 1, 2)), dma((4,)), dma((5,)),
            dma((PER, zs)), dma((PER, zs)), dma((2, n_a)), dma((2, n_a)), dma((2, ys)), dma((2, ys)),
            dma((2, n_a)), dma((2, n_a)),
        ],
        compiler_params=pltpu.CompilerParams(
            collective_id=0, has_side_effects=True, vmem_limit_bytes=56 * 2**20
        ),
        cost_estimate=pl.CostEstimate(flops=3_200_000_000, bytes_accessed=4_000_000, transcendentals=2_400_000),
        name="attention_backward",
    )(q, k, v, g, proj, hidden.T, weight, lengths)
    qg, dk, dv, down, up = pl.pallas_call(
        hand_over,
        out_shape=tuple(jax.ShapeDtypeStruct(o.shape, o.dtype) for o in outs),
        in_specs=[pl.BlockSpec(memory_space=pltpu.VMEM)] * 5,
        out_specs=(anywhere,) * 5,
        scratch_shapes=[dma((5,))],
        compiler_params=pltpu.CompilerParams(vmem_limit_bytes=8 * 2**20),
        name="hand_over",
    )(*outs)
    return qg, dk, dv, down.T, up


def solution(mesh):
    n_ctx, n_kvh = mesh.shape["ctx"], mesh.shape["kvh"]
    both = P("ctx", "kvh")
    return jax.shard_map(
        functools.partial(shards, n_ctx, n_kvh),
        mesh=mesh,
        in_specs=(both, both, both, both, both, P("ctx", None), P(None, "kvh"), P()),
        out_specs=(both, both, both, P("kvh", None), P(None, "kvh")),
        check_vma=False,
    )
```

```python
import functools
import math

import jax
import jax.numpy as jnp
from jax import lax
from jax.experimental import pallas as pl
from jax.experimental.pallas import tpu as pltpu
from jax.sharding import PartitionSpec as P

MESH = pl.DeviceIdType.MESH
HEAD = 128
HEADS = 4
BLOCK = 128
REACH = 4
TOK = 384
PER = TOK // BLOCK
SPAN = 12
ROWS = HEADS * BLOCK
NX, NCORE = 4, 2
FAR = 1e30
BF = jnp.bfloat16
F32 = jnp.float32

NT = (((1,), (1,)), ((), ()))
NN = (((1,), (0,)), ((), ()))


def dot(a, b, dims=NN):
    return lax.dot_general(a, b, dims, preferred_element_type=F32)


def fold8(tile, op):
    parts = tile.reshape(tile.shape[0] // 8, 8, tile.shape[1])
    return op(parts, axis=0)


def by_distance(n):
    return sorted(range(1, n), key=lambda o: -min(o, n - o))


def kernel(
    n_ctx, n_kvh, q_hbm, k_hbm, v_hbm, g_hbm, x_hbm, a_hbm, w_hbm, len_hbm,
    qg_ref, dk_ref, dv_ref, down_out, up_out,
    q_ref, g_ref, x_ref, a_ref, w_ref, len_ref, kwin, vwin, relay, kwin_t, s_ref, dp_ref, p_ref, ds_ref,
    top_ref, level_ref, sum_ref, near, back, got,
    mix_own, mix_send, mix_got,
    down_own, up_own, down_send, up_send, down_a, up_a, down_y, up_y, down_fin, up_fin,
    in_sem, halo_s, halo_r, back_s, back_r, mix_s, mix_r, rs_s, rs_r, ys_s, ys_r, ag_s, ag_r,
):
    n_y = n_ctx // (NX * NCORE)
    c = lax.axis_index("ctx")
    z = lax.axis_index("kvh")
    core = lax.rem(c, NCORE)
    x = lax.rem(c // NCORE, NX)
    y = c // (NX * NCORE)

    def at(yy, xx, cc):
        return ((yy * NX + xx) * NCORE + cc, z)

    def along(d):
        return (lax.rem(c + d + n_ctx, n_ctx), z)

    z_peers = [s + (s >= z).astype(jnp.int32) for s in range(n_kvh - 1)]
    y_peers = [s + (s >= y).astype(jnp.int32) for s in range(n_y - 1)]
    a_peers = [
        (lax.rem(x + dx, NX), lax.rem(core + dc, NCORE)) for dx in by_distance(NX) for dc in range(NCORE)
    ] + [(x, 1 - core)]

    own = pl.ds(REACH * TOK, TOK)
    local = [
        pltpu.make_async_copy(src, dst, in_sem.at[i])
        for i, (src, dst) in enumerate([
            (q_hbm, q_ref), (k_hbm, kwin.at[own]), (g_hbm, g_ref), (v_hbm, vwin.at[own]),
            (len_hbm, len_ref), (w_hbm, w_ref), (a_hbm, a_ref), (x_hbm, x_ref),
        ])
    ]
    lq, lk, lg, lv, llen, lw, la, lx = local

    barrier = pltpu.get_barrier_semaphore()
    greet = [along(d) for d in (1, 3, 6, -1, -3, -6)]
    greet += [(c, zz) for zz in z_peers]
    greet += [at(yy, x, core) for yy in y_peers]
    greet += [at(y, xx, cc) for xx, cc in a_peers]
    for who in greet:
        pl.semaphore_signal(barrier, inc=1, device_id=who, device_id_type=MESH)
    for cp in local:
        cp.start()
    pl.semaphore_wait(barrier, len(greet))

    mate = along(1 - 2 * core)
    first_core, second_core = core == 0, core == 1

    def slot_rows(d, first=0):
        return pl.ds((REACH - d) * TOK + first, TOK - first)

    def forward(n, j, src, d, to, first=0):
        return pltpu.make_async_remote_copy(
            src_ref=src, dst_ref=(kwin, vwin)[j].at[slot_rows(d, first)],
            send_sem=halo_s.at[n, j], recv_sem=halo_r.at[d - 1, j], device_id=to, device_id_type=MESH,
        )

    def held(j, d, first=0):
        return (kwin, vwin)[j].at[slot_rows(d, first)]

    def own_to(j, d):
        return forward(d // 2, j, (k_hbm, v_hbm)[j], d, along(d))

    def own_round(j):
        return pltpu.make_async_remote_copy(
            src_ref=(k_hbm, v_hbm)[j].at[pl.ds(BLOCK, TOK - BLOCK)], dst_ref=relay.at[j],
            send_sem=halo_s.at[2, j], recv_sem=halo_r.at[REACH, j],
            device_id=at(y, lax.rem(x + NX - 1, NX), core), device_id_type=MESH,
        )

    def pass_round(j):
        to = along(jnp.where(x == NX - 1, -2, 6))
        return forward(5, j, relay.at[j], REACH, to, BLOCK)

    def pass_mate(j, d):
        return forward(3, j, held(j, d), 2, mate)

    def pass_last(j):
        return forward(4, j, held(j, 3, BLOCK), REACH, mate, BLOCK)

    def arrived(j, d):
        first = BLOCK if d == REACH else 0
        forward(0, j, held(j, d, first), d, along(1), first).wait_recv()

    @pl.when(first_core)
    def _():
        for d, j in ((3, 0), (1, 0), (3, 1), (1, 1)):
            own_to(j, d).start()
            if d == 3:
                own_round(j).start()

    @pl.when(second_core)
    def _():
        for d, j in ((1, 0), (1, 1), (3, 0), (3, 1)):
            own_to(j, d).start()

    llen.wait()
    firsts = [jnp.int32(0)] * PER
    start = jnp.int32(0)
    for doc in range(len_hbm.shape[0]):
        for i in range(PER):
            firsts[i] = jnp.where(start <= c * PER + i, start, firsts[i])
        start = start + len_ref[doc]

    def away(i, slot):
        block = c * PER + i + slot - (SPAN - 1)
        return jnp.where(block >= firsts[i], 0.0, FAR).astype(F32)

    def rows_of(ref, i):
        return jnp.concatenate(
            [ref[i * BLOCK:(i + 1) * BLOCK, h * HEAD:(h + 1) * HEAD] for h in range(HEADS)], axis=0
        )

    for i in range(PER):
        top_ref[i] = jnp.full((8, ROWS), -2.0 * FAR, F32)

    causal = (
        lax.broadcasted_iota(jnp.int32, (BLOCK, ROWS), 0)
        <= lax.broadcasted_iota(jnp.int32, (BLOCK, ROWS), 1) % BLOCK
    )

    def window(d, i):
        low = (REACH - d) * PER
        return max(low, i + 1), min(low + PER, i + SPAN + 1)

    def scores(d):
        for i in range(PER):
            lo, hi = window(d, i)
            if lo >= hi:
                continue
            s = dot(kwin[lo * BLOCK:hi * BLOCK], rows_of(q_ref, i), NT)
            top = top_ref[i]
            for w in range(lo, hi):
                slot = w - i - 1
                tile = s[(w - lo) * BLOCK:(w - lo + 1) * BLOCK]
                if slot == SPAN - 1:
                    tile = jnp.where(causal, tile, -FAR)
                s_ref[i, slot * BLOCK:(slot + 1) * BLOCK] = tile
                top = jnp.maximum(top, fold8(tile, jnp.max) - away(i, slot))
            top_ref[i] = top
        low = (REACH - d) * TOK + (BLOCK if d == REACH else 0)
        high = (REACH - d + 1) * TOK
        kwin_t[:, low:high] = kwin[low:high].T

    def dprobs(d):
        for i in range(PER):
            lo, hi = window(d, i)
            if lo >= hi:
                continue
            dp_ref[i, (lo - i - 1) * BLOCK:(hi - i - 1) * BLOCK] = dot(
                vwin[lo * BLOCK:hi * BLOCK], rows_of(g_ref, i), NT
            )

    factor = HEAD ** -0.5
    rate = factor * math.log2(math.e)
    STEP = 64
    zero = jnp.zeros((8, ROWS), F32)

    def weights(d):
        for i in range(PER):
            lo, hi = window(d, i)
            if lo >= hi:
                continue
            top = jnp.max(top_ref[i], axis=0, keepdims=True)
            level_ref[d, i] = jnp.broadcast_to(top, (8, ROWS))
            total, delta = zero, zero
            for w in range(lo, hi):
                slot = w - i - 1
                level = top + away(i, slot)

                def weigh(t, carry, i=i, slot=slot, level=level):
                    total, delta = carry
                    span = pl.ds(pl.multiple_of(slot * BLOCK + t * STEP, STEP), STEP)
                    p = jnp.exp2((s_ref[i, span] - level) * rate)
                    s_ref[i, span] = p
                    return total + fold8(p, jnp.sum), delta + fold8(p * dp_ref[i, span], jnp.sum)

                total, delta = lax.fori_loop(0, BLOCK // STEP, weigh, (total, delta), unroll=True)
            sum_ref[d, i, 0] = total
            sum_ref[d, i, 1] = delta

    def attend(d):
        scores(d)
        dprobs(d)
        weights(d)

    lq.wait()
    lk.wait()
    lg.wait()
    lv.wait()
    attend(0)

    @pl.when(second_core)
    def _():
        for j in range(2):
            arrived(j, 1)
        attend(1)
        for j in range(2):
            arrived(j, 3)
            pass_mate(j, 3).start()
        attend(3)

    @pl.when(first_core)
    def _():
        for j in range(2):
            arrived(j, 1)
            pass_mate(j, 1).start()
        for j in range(2):
            own_round(j).wait_recv()
            pass_round(j).start()
        attend(1)

    for j in range(2):
        arrived(j, 2)
    attend(2)

    @pl.when(first_core)
    def _():
        for j in range(2):
            arrived(j, 3)
            pass_last(j).start()
        attend(3)

    mix_copies = []

    def mix_copy(i, s):
        slot = z - (z > z_peers[s]).astype(jnp.int32)
        return pltpu.make_async_remote_copy(
            src_ref=mix_send.at[i], dst_ref=mix_got.at[i, slot],
            send_sem=mix_s.at[i, s], recv_sem=mix_r.at[i, slot],
            device_id=(c, z_peers[s]), device_id_type=MESH,
        )

    def mix_arrived(i, s):
        pltpu.make_async_remote_copy(
            src_ref=mix_send.at[i], dst_ref=mix_got.at[i, s],
            send_sem=mix_s.at[i, s], recv_sem=mix_r.at[i, s],
            device_id=(c, z_peers[s]), device_id_type=MESH,
        ).wait_recv()

    def finish(i):
        top = jnp.max(top_ref[i], axis=0, keepdims=True)
        near_ranges = [d for d in range(REACH + 1) if window(d, i)[0] < window(d, i)[1]]
        fades = {d: jnp.exp2((level_ref[d, i, :1] - top) * rate) for d in near_ranges}
        total, delta = zero, zero
        for d in near_ranges:
            total = total + sum_ref[d, i, 0] * fades[d]
            delta = delta + sum_ref[d, i, 1] * fades[d]
        share = 1.0 / jnp.sum(total, axis=0, keepdims=True)
        delta = jnp.sum(delta, axis=0, keepdims=True) * share
        for d in near_ranges:
            lo, hi = window(d, i)
            start = (lo - i - 1) * BLOCK
            part = fades[d] * share
            level_ref[d, i] = jnp.broadcast_to(part, (8, ROWS))

            def settle(t, carry, i=i, start=start, part=part, delta=delta):
                span = pl.ds(pl.multiple_of(start + t * STEP, STEP), STEP)
                p = s_ref[i, span] * part
                ds_ref[i, span] = (p * (dp_ref[i, span] - delta)).astype(BF)
                return carry

            lax.fori_loop(0, (hi - lo) * BLOCK // STEP, settle, 0, unroll=True)
        dq = dot(kwin_t[:, (i + 1) * BLOCK:(i + 1 + SPAN) * BLOCK], ds_ref[i]) * factor
        for h in range(HEADS):
            qg_ref[i * BLOCK:(i + 1) * BLOCK, h * HEAD:(h + 1) * HEAD] = (
                dq[:, h * HEAD:(h + 1) * HEAD].T.astype(BF)
            )
        mixed = dot(w_ref[...], qg_ref[i * BLOCK:(i + 1) * BLOCK], NT)
        mix_own[:, i * BLOCK:(i + 1) * BLOCK] = mixed
        mix_send[i] = mixed.astype(BF)
        for n in range(n_kvh - 1):
            cp = mix_copy(i, n)
            cp.start()
            mix_copies.append(cp)

    lw.wait()
    finish(2)
    for j in range(2):
        arrived(j, REACH)
    attend(REACH)
    finish(1)
    finish(0)

    def chunk(ref, xx, cc):
        width = ref.shape[1] // NCORE
        return ref.at[pl.ds(pl.multiple_of(xx * 16, 16), 16), pl.ds(pl.multiple_of(cc * width, 128), width)]

    def scatter(which, send, got):
        copies = []
        for o, (xx, cc) in enumerate(a_peers):
            cp = pltpu.make_async_remote_copy(
                src_ref=chunk(send, xx, cc), dst_ref=got.at[o],
                send_sem=rs_s.at[which, o], recv_sem=rs_r.at[which, o],
                device_id=at(y, xx, cc), device_id_type=MESH,
            )
            cp.start()
            copies.append(cp)
        return copies

    def y_copy(which, o, mark, slots):
        return pltpu.make_async_remote_copy(
            src_ref=slots.at[y], dst_ref=slots.at[y],
            send_sem=ys_s.at[which, o], recv_sem=ys_r.at[which, mark],
            device_id=at(y_peers[o], x, core), device_id_type=MESH,
        )

    def exchange(which, copies, own_part, got, slots):
        for cp in copies:
            cp.wait_recv()
        part = chunk(own_part, x, core)[...]
        for o in range(len(a_peers)):
            part = part + got[o].astype(F32)
        slots[y] = part.astype(BF)
        out = []
        for o in range(n_y - 1):
            cp = y_copy(which, o, y - (y > y_peers[o]).astype(jnp.int32), slots)
            cp.start()
            out.append(cp)
        return out

    def gather(which, slots, fin):
        for o in range(n_y - 1):
            y_copy(which, o, o, slots).wait_recv()
        part = slots[0].astype(F32)
        for yy in range(1, n_y):
            part = part + slots[yy].astype(F32)
        mine = chunk(fin, x, core)
        mine[...] = part.astype(BF)
        out = []
        for o, (xx, cc) in enumerate(a_peers):
            cp = pltpu.make_async_remote_copy(
                src_ref=mine, dst_ref=mine,
                send_sem=ag_s.at[which, o], recv_sem=ag_r.at[which, o],
                device_id=at(y, xx, cc), device_id_type=MESH,
            )
            cp.start()
            out.append(cp)
        return out

    la.wait()
    up = dot(a_ref[...], qg_ref[...])
    up_own[...] = up
    up_send[...] = up.astype(BF)
    up_rs = scatter(0, up_send, up_a)

    def ranges(d):
        for i in range(PER):
            lo, hi = window(d, i)
            if lo >= hi:
                continue
            start = (lo - i - 1) * BLOCK
            part = level_ref[d, i, :1]

            def normal(t, carry, i=i, start=start, part=part):
                span = pl.ds(pl.multiple_of(start + t * STEP, STEP), STEP)
                p_ref[i, span] = (s_ref[i, span] * part).astype(BF)
                return carry

            lax.fori_loop(0, (hi - lo) * BLOCK // STEP, normal, 0)
        low = (REACH - d) * PER
        dk = jnp.zeros((TOK, HEAD), F32)
        dv = jnp.zeros((TOK, HEAD), F32)
        parts_k, parts_v = [None] * PER, [None] * PER
        for i in range(PER):
            lo, hi = window(d, i)
            if lo >= hi:
                continue
            span = slice((lo - i - 1) * BLOCK, (hi - i - 1) * BLOCK)
            k_part = dot(ds_ref[i, span], rows_of(q_ref, i))
            v_part = dot(p_ref[i, span], rows_of(g_ref, i))
            for w in range(lo, hi):
                at_w = slice((w - lo) * BLOCK, (w - lo + 1) * BLOCK)
                b = w - low
                parts_k[b] = k_part[at_w] if parts_k[b] is None else parts_k[b] + k_part[at_w]
                parts_v[b] = v_part[at_w] if parts_v[b] is None else parts_v[b] + v_part[at_w]
        return parts_k, parts_v

    def store(d):
        parts = ranges(d)
        first = BLOCK if d == REACH else 0
        for j in range(2):
            for b in range(first // BLOCK, PER):
                value = parts[j][b] * factor if j == 0 else parts[j][b]
                near[d, j, b * BLOCK:(b + 1) * BLOCK] = value.astype(near.dtype)

    def send_back(n, src, slot, to, first=0):
        rows = pl.ds(first, TOK - first)
        return pltpu.make_async_remote_copy(
            src_ref=src.at[:, rows], dst_ref=got.at[slot, :, rows],
            send_sem=back_s.at[n], recv_sem=back_r.at[slot], device_id=to, device_id_type=MESH,
        )

    def came_back(slot, first=0):
        send_back(0, got.at[slot], slot, along(-1), first).wait_recv()

    back_4 = send_back(0, back.at[0], 0, along(-1), BLOCK)
    back_2 = send_back(1, back.at[1], 1, mate)
    back_1 = send_back(2, back.at[2], 2, along(-1))
    back_3 = send_back(2, back.at[2], 3, along(-2))
    last_0 = send_back(3, back.at[3], 4, along(-1))
    last_1 = send_back(3, back.at[3], 4, along(-3))

    store(REACH)
    back[0, :, BLOCK:] = near[REACH, :, BLOCK:].astype(BF)
    back_4.start()
    store(3)

    @pl.when(first_core)
    def _():
        came_back(0, BLOCK)
        back[2, :, :BLOCK] = near[3, :, :BLOCK].astype(BF)
        back[2, :, BLOCK:] = (near[3, :, BLOCK:] + got[0, :, BLOCK:].astype(F32)).astype(BF)
        back_3.start()

    store(2)
    back[1] = near[2].astype(BF)
    back_2.start()
    store(1)

    @pl.when(second_core)
    def _():
        back[2] = near[1].astype(BF)
        back_1.start()

    store(0)
    up_ys = exchange(0, up_rs, up_own, up_a, up_y)

    lx.wait()
    for i in range(PER - 1, -1, -1):
        cols = slice(i * BLOCK, (i + 1) * BLOCK)
        mixed = mix_own[:, cols]
        for n in range(n_kvh - 1):
            mix_arrived(i, n)
            mixed = mixed + mix_got[i, n].astype(F32)
        part = dot(mixed.astype(BF), x_ref[cols])
        if i < PER - 1:
            part = part + down_own[...]
        down_own[...] = part
        if i == 0:
            down_send[...] = part.astype(BF)
    down_rs = scatter(1, down_send, down_a)
    down_ys = exchange(1, down_rs, down_own, down_a, down_y)

    came_back(1)

    @pl.when(first_core)
    def _():
        came_back(3)
        back[3] = (near[1] + got[1].astype(F32) + got[3].astype(F32)).astype(BF)
        last_0.start()

    @pl.when(second_core)
    def _():
        came_back(0, BLOCK)
        back[3, :, :BLOCK] = (near[3, :, :BLOCK] + got[1, :, :BLOCK].astype(F32)).astype(BF)
        back[3, :, BLOCK:] = (
            near[3, :, BLOCK:] + got[1, :, BLOCK:].astype(F32) + got[0, :, BLOCK:].astype(F32)
        ).astype(BF)
        last_1.start()

    up_ag = gather(0, up_y, up_fin)
    down_ag = gather(1, down_y, down_fin)

    @pl.when(first_core)
    def _():
        came_back(2)
        near[0] = near[0] + got[2].astype(F32)

    came_back(4)
    dk_ref[...] = (near[0, 0] + got[4, 0].astype(F32)).astype(BF)
    dv_ref[...] = (near[0, 1] + got[4, 1].astype(F32)).astype(BF)

    scale = (TOK * n_ctx) ** -0.5
    for cp in up_ag:
        cp.wait_recv()
    up_out[...] = up_fin[...].astype(F32) * scale
    for cp in down_ag:
        cp.wait_recv()
    down_out[...] = down_fin[...].astype(F32) * scale

    @pl.when(first_core)
    def _():
        for j in range(2):
            own_round(j).wait_send()
            pass_round(j).wait_send()
            pass_mate(j, 1).wait_send()
            pass_last(j).wait_send()
        back_3.wait_send()
        last_0.wait_send()

    @pl.when(second_core)
    def _():
        for j in range(2):
            pass_mate(j, 3).wait_send()
        back_1.wait_send()
        last_1.wait_send()

    for j in range(2):
        own_to(j, 1).wait_send()
        own_to(j, 3).wait_send()
    back_4.wait_send()
    back_2.wait_send()
    for group in (mix_copies, up_rs, down_rs, up_ys, down_ys, up_ag, down_ag):
        for cp in group:
            cp.wait_send()


def hand_over(*refs):
    arrays, results, sem = refs[:5], refs[5:10], refs[10]
    out = [pltpu.make_async_copy(arrays[i], results[i], sem.at[i]) for i in range(5)]
    for cp in out:
        cp.start()
    for cp in out:
        cp.wait()


def shards(n_ctx, n_kvh, q, k, v, g, proj, hidden, weight, lengths):
    n_y = n_ctx // (NX * NCORE)
    n_a = NX * NCORE - 1
    feats, rank = proj.shape[1], hidden.shape[1]
    wide = q.shape[1]
    vm = pltpu.VMEM
    dma = pltpu.SemaphoreType.DMA
    win = (REACH + 1) * TOK
    anywhere = pl.BlockSpec(memory_space=pl.ANY)
    zs, ys = max(n_kvh - 1, 1), max(n_y - 1, 1)
    outs = pl.pallas_call(
        functools.partial(kernel, n_ctx, n_kvh),
        out_shape=(
            pltpu.VMEM(q.shape, BF),
            pltpu.VMEM(k.shape, BF),
            pltpu.VMEM(v.shape, BF),
            pltpu.VMEM((rank, feats), F32),
            pltpu.VMEM((rank, wide), F32),
        ),
        in_specs=[anywhere] * 8,
        out_specs=(pl.BlockSpec(memory_space=pltpu.VMEM),) * 5,
        scratch_shapes=[
            vm(q.shape, BF), vm(g.shape, BF), vm(proj.shape, BF), vm((rank, TOK), BF), vm(weight.shape, BF),
            pltpu.SMEM(lengths.shape, jnp.int32),
            vm((win, HEAD), BF), vm((win, HEAD), BF), vm((2, TOK - BLOCK, HEAD), BF), vm((HEAD, win), BF),
            vm((PER, SPAN * BLOCK, ROWS), F32), vm((PER, SPAN * BLOCK, ROWS), F32),
            vm((PER, SPAN * BLOCK, ROWS), BF), vm((PER, SPAN * BLOCK, ROWS), BF),
            vm((PER, 8, ROWS), F32), vm((REACH + 1, PER, 8, ROWS), F32), vm((REACH + 1, PER, 2, 8, ROWS), F32),
            vm((REACH + 1, 2, TOK, HEAD), F32), vm((4, 2, TOK, HEAD), BF), vm((5, 2, TOK, HEAD), BF),
            vm((rank, TOK), F32), vm((PER, rank, BLOCK), BF), vm((PER, zs, rank, BLOCK), BF),
            vm((rank, feats), F32), vm((rank, wide), F32), vm((rank, feats), BF), vm((rank, wide), BF),
            vm((n_a, 16, feats // NCORE), BF), vm((n_a, 16, wide // NCORE), BF),
            vm((n_y, 16, feats // NCORE), BF), vm((n_y, 16, wide // NCORE), BF),
            vm((rank, feats), BF), vm((rank, wide), BF),
            dma((8,)), dma((6, 2)), dma((REACH + 1, 2)), dma((4,)), dma((5,)),
            dma((PER, zs)), dma((PER, zs)), dma((2, n_a)), dma((2, n_a)), dma((2, ys)), dma((2, ys)),
            dma((2, n_a)), dma((2, n_a)),
        ],
        compiler_params=pltpu.CompilerParams(
            collective_id=0, has_side_effects=True, vmem_limit_bytes=56 * 2**20
        ),
        cost_estimate=pl.CostEstimate(flops=3_200_000_000, bytes_accessed=4_000_000, transcendentals=2_400_000),
        name="attention_backward",
    )(q, k, v, g, proj, hidden.T, weight, lengths)
    qg, dk, dv, down, up = pl.pallas_call(
        hand_over,
        out_shape=tuple(jax.ShapeDtypeStruct(o.shape, o.dtype) for o in outs),
        in_specs=[pl.BlockSpec(memory_space=pltpu.VMEM)] * 5,
        out_specs=(anywhere,) * 5,
        scratch_shapes=[dma((5,))],
        compiler_params=pltpu.CompilerParams(vmem_limit_bytes=8 * 2**20),
        name="hand_over",
    )(*outs)
    return qg, dk, dv, down.T, up


def solution(mesh):
    n_ctx, n_kvh = mesh.shape["ctx"], mesh.shape["kvh"]
    both = P("ctx", "kvh")
    return jax.shard_map(
        functools.partial(shards, n_ctx, n_kvh),
        mesh=mesh,
        in_specs=(both, both, both, both, both, P("ctx", None), P(None, "kvh"), P()),
        out_specs=(both, both, both, P("kvh", None), P(None, "kvh")),
        check_vma=False,
    )
```
